256 devices in a mesh: rows: 64 (over x, z, core), grp: 4 (over y).
Axes of the slice: x: 4, y: 4, z: 8, core: 2. Of those that a mesh axis runs over, the one named last changes fastest.
Arguments:
- matrix: bfloat16 [524288, 256], P(('grp', 'rows'))
- signs: int32 [524288], P(('grp', 'rows')), may hold values from -1 to 1, as said below
- picks: int32 [16384], P(('grp', 'rows')), may hold values from 0 to 524287, as said below
Outputs:
- sketch: float32 [16384, 256], P(('grp', 'rows'))
- factor: float32 [256, 256], replicated
The draws below stay inside these ranges and needn't reach their ends.
Inputs may be any that keep to these rules, and one draw needn't show every extreme that they name: `signs`: each entry is +1 or -1. `picks`: the indices are distinct, and the 64 indices of block b (positions b * 64 to (b + 1) * 64 - 1) lie in rows b * 2048 to (b + 1) * 2048 - 1.
All inputs are finite; a program needn't handle non-finite values.
Results may differ from the reference program's by a relative error of at most 0.0003.
Values sent between devices are 32-bit elements; how exact they have to be, the bound alone decides.
No kernel may reach another device: no remote copies, remote signals or barrier semaphores. Data moves between devices by JAX's collectives and lax.ppermute only.
A program may use at most 64 MiB of HBM per device.

```python
import math
import jax
import jax.numpy as jnp
from jax import lax

W = 256
BLOCK = 128
ROWS_DEV = 2048
SAMP_DEV = 64
TOTAL_ROWS = 524288
SAMPLES = 16384


def draw_matrix(key, part):
    key = jax.random.fold_in(key, 11)
    keys = jax.random.split(key, 5)
    noise = jax.random.normal(keys[0], (TOTAL_ROWS, W), jnp.float32)
    low_row, high_row = (0.2, 2.0)
    row_scale = jnp.exp(jax.random.uniform(keys[1], (TOTAL_ROWS,), jnp.float32, jnp.log(low_row), jnp.log(high_row)))
    column_scale = jnp.exp(jax.random.uniform(keys[2], (W,), jnp.float32, jnp.log(0.3), jnp.log(3.0)))
    common_row = jax.random.normal(keys[3], (TOTAL_ROWS,), jnp.float32)
    common_column = 0.7 * jax.random.normal(keys[4], (W,), jnp.float32)
    values = row_scale[:, None] * (noise * column_scale[None, :] + common_row[:, None] * common_column[None, :])
    return values.astype(jnp.bfloat16)


def draw_signs(key, part):
    key = jax.random.fold_in(key, 23)
    return 2 * jax.random.randint(key, (TOTAL_ROWS,), 0, 2, jnp.int32) - 1


def draw_picks(key, part):
    key = jax.random.fold_in(key, 37)
    count = TOTAL_ROWS // ROWS_DEV
    keys = jax.random.split(key, count)
    chosen = jax.vmap(lambda single: jax.random.permutation(single, ROWS_DEV))(keys)[:, :SAMP_DEV].astype(jnp.int32)
    first = chosen[0]
    first = jnp.where(first == 0, first[0], first).at[0].set(0)
    final = chosen[count - 1]
    final = jnp.where(final == ROWS_DEV - 1, final[SAMP_DEV - 1], final).at[SAMP_DEV - 1].set(ROWS_DEV - 1)
    chosen = chosen.at[0].set(first).at[count - 1].set(final)
    offsets = jnp.arange(count, dtype=jnp.int32) * ROWS_DEV
    return (chosen + offsets[:, None]).reshape(-1)


def setup_inputs(seed: int = 0) -> dict:
    key_of = jax.random.split(jax.random.key(seed), 4)
    matrix = draw_matrix(jax.random.fold_in(key_of[3], 71), 0)
    signs = draw_signs(jax.random.fold_in(key_of[3], 71), 0)
    picks = draw_picks(jax.random.fold_in(key_of[3], 71), 0)
    return dict(matrix=matrix, signs=signs, picks=picks)


def sylvester(order, dtype):
    index = jnp.arange(order, dtype=jnp.int32)
    both = jnp.bitwise_and(index[:, None], index[None, :])
    parity = jnp.zeros((order, order), jnp.int32)
    for place in range(order.bit_length()):
        parity = parity + jnp.bitwise_and(jnp.right_shift(both, place), 1)
    return (1 - 2 * (parity % 2)).astype(dtype)

def reference(matrix, signs, picks):
    signed = matrix * signs.astype(jnp.bfloat16)[:, None]
    outer = TOTAL_ROWS // BLOCK
    table = sylvester(BLOCK, jnp.float32)
    blocks = signed.reshape(outer, BLOCK, W).astype(jnp.float32)
    current = jnp.einsum('ij,ojw->oiw', table, blocks, precision=lax.Precision.HIGHEST)
    half = 1
    while half < outer:
        shaped = current.reshape(outer // (2 * half), 2, half, BLOCK, W)
        current = jnp.stack([shaped[:, 0] + shaped[:, 1], shaped[:, 0] - shaped[:, 1]], axis=1)
        current = current.reshape(outer, BLOCK, W)
        half = half * 2
    transformed = current.reshape(TOTAL_ROWS, W) / math.sqrt(TOTAL_ROWS)
    sketch = transformed[picks]
    gram = jnp.dot(sketch.T.astype(jnp.float32), sketch.astype(jnp.float32), precision=lax.Precision.HIGHEST, preferred_element_type=jnp.float32) / SAMPLES
    factor = jnp.linalg.cholesky(gram).T
    return (sketch, factor)
```

```python
import math

import jax
import jax.numpy as jnp
from jax import lax
from jax.experimental import pallas as pl
from jax.experimental.pallas import tpu as pltpu
from jax.sharding import Mesh, PartitionSpec as P

NX, NZH, NZ0, NC, NY = 4, 4, 2, 2, 4
NZ = NZH * NZ0
NQ = NX * NY
ROWS = 2048
SAMP = 64
OUTER = 8
ORDER = 256
W = 256
GROUP = NC * NZ0 * NX * NY
COLS = W // GROUP
CHUNK = OUTER * 8 + 2
CHIPS = NZH * NZ0 * NX * NY
LANES = 128
F32 = jnp.float32
HIGHEST = lax.Precision.HIGHEST
VMEM = pl.BlockSpec(memory_space=pltpu.VMEM)
SMEM = pl.BlockSpec(memory_space=pltpu.SMEM)


def params(mib):
    return pltpu.CompilerParams(vmem_limit_bytes=mib * 1024 * 1024)


def shape(*sizes):
    return jax.ShapeDtypeStruct(sizes, F32)


def parity_sign(value):
    return (1 - 2 * ((value ^ (value >> 1)) & 1)).astype(F32)


def butterfly(values):
    values = list(values)
    half = 1
    while half < len(values):
        for first in range(len(values)):
            if first & half == 0:
                a, b = values[first], values[first | half]
                values[first], values[first | half] = a + b, a - b
        half *= 2
    return values


def total(parts):
    while len(parts) > 1:
        parts = [parts[k] + parts[k + 1] for k in range(0, len(parts), 2)]
    return parts[0]


def local_kernel(matrix, signs, table):
    row = lax.broadcasted_iota(jnp.int32, (ORDER, ORDER), 0)
    col = lax.broadcasted_iota(jnp.int32, (ORDER, ORDER), 1)
    both = row & col
    both = both ^ (both >> 4)
    both = both ^ (both >> 2)
    both = both ^ (both >> 1)
    hadamard = (1 - 2 * (both & 1)).astype(F32).astype(jnp.bfloat16)
    for o in range(OUTER):
        block = matrix[o * ORDER : (o + 1) * ORDER, :].astype(F32)
        sign = jnp.concatenate([signs[2 * o : 2 * o + 1, :], signs[2 * o + 1 : 2 * o + 2, :]], axis=1)
        flipped = (block.T * sign.astype(F32)).astype(jnp.bfloat16)
        table[o] = jnp.dot(flipped, hadamard, preferred_element_type=F32)


def pack_kernel(ids, table, p0, p1, p2, p3, out):
    zh = ids[0]
    sub = lax.broadcasted_iota(jnp.int32, (8, LANES), 0)
    for o in range(OUTER):
        for pair in range(GROUP // 2):
            low = table[o, pair * 8 : pair * 8 + 8, :LANES]
            high = table[o, pair * 8 : pair * 8 + 8, LANES:]
            spot = 2 * pair * CHUNK + o * 8
            out[spot : spot + 8, :] = jnp.where(sub < 4, low, pltpu.roll(high, 4, 0))
            spot += CHUNK
            out[spot : spot + 8, :] = jnp.where(sub < 4, pltpu.roll(low, 4, 0), high)
    row = lax.broadcasted_iota(jnp.int32, (2, LANES), 0)
    lane = lax.broadcasted_iota(jnp.int32, (2, LANES), 1)
    tile = jnp.zeros((2, LANES), F32)
    for d, ref in enumerate((p0, p1, p2, p3)):
        spot = zh ^ d
        value = (ref[...] & (ROWS - 1)).astype(F32)
        value = jnp.broadcast_to(jnp.concatenate([value, value], axis=1), (2, LANES))
        here = (row == (spot >> 1)) & ((lane >> 6) == (spot & 1))
        tile = jnp.where(here, value, tile)
    for k in range(GROUP):
        out[k * CHUNK + OUTER * 8 : (k + 1) * CHUNK, :] = tile


def gather_kernel(blocks, out, table):
    for high in range(32):
        values = [blocks[(high * 2 + low) * CHUNK + o * 8 : (high * 2 + low) * CHUNK + o * 8 + 8, :] for low in range(2) for o in range(OUTER)]
        for k, value in enumerate(butterfly(values)):
            table[high * 16 + k] = value
    for rest in range(16):
        values = [table[high * 16 + rest] for high in range(32)]
        for high, value in enumerate(butterfly(values)):
            table[high * 16 + rest] = value
    sub = lax.broadcasted_iota(jnp.int32, (8, LANES), 0)
    lane = lax.broadcasted_iota(jnp.int32, (8, LANES), 1)
    upper, first = sub >= 4, lane < SAMP
    for half in range(GROUP // 4):
        for zp in range(2):
            rows = []
            for c in range(NC):
                picked = []
                for ylo in range(2):
                    device = c * (GROUP // 2) + half * 2 + ylo
                    spot = device * CHUNK + OUTER * 8 + zp
                    index = blocks[spot : spot + 1, :].astype(jnp.int32)
                    index = jnp.broadcast_to(index, (8, LANES))
                    low = index & (LANES - 1)
                    level = [
                        jnp.take_along_axis(table[device * 8 + o], low, axis=1, mode="promise_in_bounds")
                        for o in range(OUTER)
                    ]
                    for place in range(3):
                        odd = (index & (ORDER << place)) != 0
                        level = [jnp.where(odd, level[k + 1], level[k]) for k in range(0, len(level), 2)]
                    same = ((index & LANES) != 0) == upper
                    picked.append(jnp.where(same, level[0], pltpu.roll(level[0], 4, 0)))
                rows.append(jnp.where(upper, picked[1], picked[0]))
            turned = [pltpu.roll(row, SAMP, 1) for row in rows]
            out[2 * zp, half * 8 : half * 8 + 8, :] = jnp.where(first, rows[0], turned[1])
            out[2 * zp + 1, half * 8 : half * 8 + 8, :] = jnp.where(first, turned[0], rows[1])


def zsum_kernel(scale, ids, blocks, out):
    zh = ids[0]
    out[...] = total([blocks[d] * (parity_sign(zh & d) * scale) for d in range(NZH)])


def gram_kernel(ids, mine, other, sketch, gram, both, turned):
    c = ids[1]
    both[pl.ds(pl.multiple_of(c * 128, 128), 128), :] = mine[...]
    both[pl.ds(pl.multiple_of((1 - c) * 128, 128), 128), :] = other[...]
    value = both[...]
    turned[...] = value.T
    sketch[...] = turned[pl.ds(pl.multiple_of(c * SAMP, SAMP), SAMP), :]
    half = both[pl.ds(pl.multiple_of(c * 128, 128), 128), :]
    gram[...] = lax.dot_general(
        half, value, (((1,), (1,)), ((), ())), precision=HIGHEST, preferred_element_type=F32
    )


def spread_kernel(scale, blocks, out):
    value = total([blocks[k] for k in range(blocks.shape[0])]) * scale
    for k in range(out.shape[0]):
        out[k] = value


def factor_kernel(gram, factor, work):
    work[...] = gram[...]
    sub = lax.broadcasted_iota(jnp.int32, (8, LANES), 0)
    lane = lax.broadcasted_iota(jnp.int32, (8, LANES), 1)
    for m in range(W // 8):
        top, at = m * 8, m * 8 % LANES
        tiles = range(m * 8 // LANES, W // LANES)
        spans = {t: slice(t * LANES, (t + 1) * LANES) for t in tiles}
        rows = [{t: jnp.broadcast_to(work[top + k : top + k + 1, spans[t]], (8, LANES)) for t in tiles} for k in range(8)]
        head = [[None] * i + [jnp.broadcast_to(rows[i][tiles[0]][:, at + j : at + j + 1], (8, LANES)) for j in range(i, 8)] for i in range(8)]
        inverse = []
        for k in range(8):
            inverse.append(lax.rsqrt(head[k][k]))
            for j in range(k + 1, 8):
                head[k][j] = head[k][j] * inverse[k]
            for t in tiles:
                rows[k][t] = rows[k][t] * inverse[k]
            for i in range(k + 1, 8):
                for j in range(i, 8):
                    head[i][j] = head[i][j] - head[k][i] * head[k][j]
                for t in tiles:
                    rows[i][t] = rows[i][t] - head[k][i] * rows[k][t]
        for t in range(W // LANES):
            if t not in spans:
                factor[top : top + 8, t * LANES : (t + 1) * LANES] = jnp.zeros((8, LANES), F32)
                continue
            value = rows[0][t]
            for k in range(1, 8):
                value = jnp.where(sub == k, rows[k][t], value)
            if t == tiles[0]:
                value = jnp.where(lane - at >= sub, value, 0.0)
            factor[top : top + 8, spans[t]] = value
        solved = [None] * 8
        for k in reversed(range(8)):
            solved[k] = {}
            for t in tiles:
                value = rows[k][t]
                for i in range(7, k, -1):
                    value = value - head[k][i] * solved[i][t]
                solved[k][t] = value * inverse[k]
        for g in range(m + 1, W // 8):
            block = work[g * 8 : g * 8 + 8, spans[tiles[0]]]
            sides = [jnp.broadcast_to(block[:, at + j : at + j + 1], (8, LANES)) for j in range(8)]
            for t in tiles:
                if m % 16 == 15 and t == tiles[0]:
                    continue
                parts = [sides[j] * solved[j][t] for j in range(8)]
                while len(parts) > 1:
                    parts = [parts[k] + parts[k + 1] for k in range(0, len(parts), 2)]
                work[g * 8 : g * 8 + 8, spans[t]] = work[g * 8 : g * 8 + 8, spans[t]] - parts[0]


def on_device(matrix, signs, picks):
    zh, c = lax.axis_index("zh"), lax.axis_index("core")
    ids = jnp.stack([zh, c]).astype(jnp.int32)
    line = [picks] + [lax.ppermute(picks, "zh", [(i, i ^ d) for i in range(NZH)]) for d in range(1, NZH)]
    line = [value.reshape(1, SAMP) for value in line]

    table = pl.pallas_call(
        local_kernel,
        out_shape=shape(OUTER, W, ORDER),
        in_specs=[VMEM, VMEM],
        out_specs=VMEM,
        compiler_params=params(16),
        name="local",
    )(matrix, signs.reshape(OUTER * 2, LANES))
    packed = pl.pallas_call(
        pack_kernel,
        out_shape=shape(GROUP * CHUNK, LANES),
        in_specs=[SMEM] + [VMEM] * 5,
        out_specs=VMEM,
        compiler_params=params(16),
        name="pack",
    )(ids, table, *line)
    packed = packed.reshape(GROUP, CHUNK // 2, 2, LANES)
    packed = lax.all_to_all(packed, ("core", "z0", "x", "y"), 0, 0, tiled=True).reshape(GROUP * CHUNK, LANES)

    sampled = pl.pallas_call(
        gather_kernel,
        out_shape=shape(NZH, CHIPS // NZH * COLS, LANES),
        in_specs=[VMEM],
        out_specs=VMEM,
        scratch_shapes=[pltpu.VMEM((GROUP * OUTER, 8, LANES), F32)],
        compiler_params=params(16),
        name="gather",
    )(packed)
    sampled = lax.all_to_all(
        sampled.reshape(CHIPS, COLS, LANES), ("zh", "z0", "x", "y"), 0, 0, tiled=True
    ).reshape(NZH, CHIPS // NZH * COLS, LANES)

    mine = pl.pallas_call(
        lambda *refs: zsum_kernel(1.0 / math.sqrt(ROWS * 256), *refs),
        out_shape=shape(128, LANES),
        in_specs=[SMEM, VMEM],
        out_specs=VMEM,
        compiler_params=params(4),
        name="zsum",
    )(ids, sampled)
    other = lax.ppermute(mine, "core", [(0, 1), (1, 0)])
    sketch, gram = pl.pallas_call(
        gram_kernel,
        out_shape=[shape(SAMP, W), shape(W // NC, W)],
        in_specs=[SMEM, VMEM, VMEM],
        out_specs=[VMEM, VMEM],
        scratch_shapes=[pltpu.VMEM((W, 128), F32), pltpu.VMEM((128, W), F32)],
        compiler_params=params(4),
        name="gram",
    )(ids, mine, other)

    def spread(blocks, count, scale, name):
        return pl.pallas_call(
            lambda *refs: spread_kernel(scale, *refs),
            out_shape=shape(count, 8, W),
            in_specs=[VMEM],
            out_specs=VMEM,
            compiler_params=params(4),
            name=name,
        )(blocks)

    gram = lax.all_to_all(gram.reshape(NQ, 8, W), ("x", "y"), 0, 0, tiled=True)
    rows = spread(gram, NZ, 1.0, "sum_xy")
    rows = lax.all_to_all(rows, ("zh", "z0"), 0, 0, tiled=True)
    rows = spread(rows, NC * NQ, 1.0 / (SAMP * 256), "sum_z")
    gram = lax.all_to_all(rows, ("core", "x", "y"), 0, 0, tiled=True).reshape(W, W)
    factor = pl.pallas_call(
        factor_kernel,
        out_shape=shape(W, W),
        in_specs=[VMEM],
        out_specs=VMEM,
        scratch_shapes=[pltpu.VMEM((W, W), F32)],
        compiler_params=params(4),
        name="factor",
    )(gram)
    return (sketch, factor)


def solution(mesh):
    devices = mesh.devices.transpose([mesh.axis_names.index(name) for name in ("rows", "grp")])
    split = Mesh(devices.reshape(NX, NZH, NZ0, NC, NY), ("x", "zh", "z0", "core", "y"))
    rows = ("y", "x", "zh", "z0", "core")
    return jax.shard_map(
        on_device,
        mesh=split,
        in_specs=(P(rows, None), P(rows), P(rows)),
        out_specs=(P(rows, None), P()),
        check_vma=False,
    )
```

```python
import math

import jax
import jax.numpy as jnp
from jax import lax
from jax.experimental import pallas as pl
from jax.experimental.pallas import tpu as pltpu
from jax.sharding import Mesh, PartitionSpec as P

NX, NZH, NZ0, NC, NY = 4, 4, 2, 2, 4
NZ = NZH * NZ0
NQ = NX * NY
ROWS = 2048
SAMP = 64
OUTER = 8
ORDER = 256
W = 256
GROUP = NC * NZ0 * NX * NY
COLS = W // GROUP
CHUNK = OUTER * 8 + 2
CHIPS = NZH * NZ0 * NX * NY
LANES = 128
F32 = jnp.float32
HIGHEST = lax.Precision.HIGHEST
VMEM = pl.BlockSpec(memory_space=pltpu.VMEM)
SMEM = pl.BlockSpec(memory_space=pltpu.SMEM)


def params(mib):
    return pltpu.CompilerParams(vmem_limit_bytes=mib * 1024 * 1024)


def shape(*sizes):
    return jax.ShapeDtypeStruct(sizes, F32)


def parity_sign(value):
    return (1 - 2 * ((value ^ (value >> 1)) & 1)).astype(F32)


def butterfly(values):
    values = list(values)
    half = 1
    while half < len(values):
        for first in range(len(values)):
            if first & half == 0:
                a, b = values[first], values[first | half]
                values[first], values[first | half] = a + b, a - b
        half *= 2
    return values


def total(parts):
    while len(parts) > 1:
        parts = [parts[k] + parts[k + 1] for k in range(0, len(parts), 2)]
    return parts[0]


def local_kernel(matrix, signs, table):
    row = lax.broadcasted_iota(jnp.int32, (ORDER, ORDER), 0)
    col = lax.broadcasted_iota(jnp.int32, (ORDER, ORDER), 1)
    both = row & col
    both = both ^ (both >> 4)
    both = both ^ (both >> 2)
    both = both ^ (both >> 1)
    hadamard = (1 - 2 * (both & 1)).astype(F32).astype(jnp.bfloat16)
    for o in range(OUTER):
        block = matrix[o * ORDER : (o + 1) * ORDER, :].astype(F32)
        sign = jnp.concatenate([signs[2 * o : 2 * o + 1, :], signs[2 * o + 1 : 2 * o + 2, :]], axis=1)
        flipped = (block.T * sign.astype(F32)).astype(jnp.bfloat16)
        table[o] = jnp.dot(flipped, hadamard, preferred_element_type=F32)


def pack_kernel(table, picks, out):
    sub = lax.broadcasted_iota(jnp.int32, (8, LANES), 0)
    for o in range(OUTER):
        for pair in range(GROUP // 2):
            low = table[o, pair * 8 : pair * 8 + 8, :LANES]
            high = table[o, pair * 8 : pair * 8 + 8, LANES:]
            spot = 2 * pair * CHUNK + o * 8
            out[spot : spot + 8, :] = jnp.where(sub < 4, low, pltpu.roll(high, 4, 0))
            spot += CHUNK
            out[spot : spot + 8, :] = jnp.where(sub < 4, pltpu.roll(low, 4, 0), high)
    value = (picks[...] & (ROWS - 1)).astype(F32)
    value = jnp.broadcast_to(jnp.concatenate([value, value], axis=1), (2, LANES))
    for k in range(GROUP):
        out[k * CHUNK + OUTER * 8 : (k + 1) * CHUNK, :] = value


def picks_kernel(blocks, out):
    for k in range(GROUP):
        spot = k * CHUNK + OUTER * 8
        out[k : k + 1, :] = blocks[spot : spot + 1, :].astype(jnp.int32)


def transform_kernel(blocks, table):
    for high in range(32):
        values = [
            blocks[(high * 2 + low) * CHUNK + o * 8 : (high * 2 + low) * CHUNK + o * 8 + 8, :]
            for low in range(2)
            for o in range(OUTER)
        ]
        for k, value in enumerate(butterfly(values)):
            table[high * 16 + k] = value
    for rest in range(16):
        values = [table[high * 16 + rest] for high in range(32)]
        for high, value in enumerate(butterfly(values)):
            table[high * 16 + rest] = value


def gather_kernel(ids, table, p0, p1, p2, p3, out):
    zh = ids[0]
    sub = lax.broadcasted_iota(jnp.int32, (8, LANES), 0)
    lane = lax.broadcasted_iota(jnp.int32, (8, LANES), 1)
    upper, first = sub >= 4, lane < SAMP
    for half in range(GROUP // 4):
        for d, (left, right) in enumerate(((p0, p1), (p2, p3))):
            rows = []
            for c in range(NC):
                picked = []
                for ylo in range(2):
                    device = c * (GROUP // 2) + half * 2 + ylo
                    index = jnp.where(first[:1], left[device : device + 1, :], right[device : device + 1, :])
                    index = jnp.broadcast_to(index, (8, LANES))
                    low = index & (LANES - 1)
                    level = [
                        jnp.take_along_axis(table[device * 8 + o], low, axis=1, mode="promise_in_bounds")
                        for o in range(OUTER)
                    ]
                    for place in range(3):
                        odd = (index & (ORDER << place)) != 0
                        level = [jnp.where(odd, level[k + 1], level[k]) for k in range(0, len(level), 2)]
                    same = ((index & LANES) != 0) == upper
                    picked.append(jnp.where(same, level[0], pltpu.roll(level[0], 4, 0)))
                rows.append(jnp.where(upper, picked[1], picked[0]))
            turned = [pltpu.roll(row, SAMP, 1) for row in rows]
            out[zh ^ (2 * d), half * 8 : half * 8 + 8, :] = jnp.where(first, rows[0], turned[1])
            out[zh ^ (2 * d + 1), half * 8 : half * 8 + 8, :] = jnp.where(first, turned[0], rows[1])


def zsum_kernel(scale, ids, blocks, out):
    zh = ids[0]
    out[...] = total([blocks[d] * (parity_sign(zh & d) * scale) for d in range(NZH)])


def gram_kernel(ids, mine, other, sketch, gram, both, turned):
    c = ids[1]
    both[pl.ds(pl.multiple_of(c * 128, 128), 128), :] = mine[...]
    both[pl.ds(pl.multiple_of((1 - c) * 128, 128), 128), :] = other[...]
    value = both[...]
    turned[...] = value.T
    sketch[...] = turned[pl.ds(pl.multiple_of(c * SAMP, SAMP), SAMP), :]
    half = both[pl.ds(pl.multiple_of(c * 128, 128), 128), :]
    gram[...] = lax.dot_general(
        half, value, (((1,), (1,)), ((), ())), precision=HIGHEST, preferred_element_type=F32
    )


def spread_kernel(scale, blocks, out):
    value = total([blocks[k] for k in range(blocks.shape[0])]) * scale
    for k in range(out.shape[0]):
        out[k] = value


def factor_kernel(gram, factor, work):
    work[...] = gram[...]
    sub = lax.broadcasted_iota(jnp.int32, (8, LANES), 0)
    lane = lax.broadcasted_iota(jnp.int32, (8, LANES), 1)
    block = 32
    for top in range(0, W, 8):
        at, tile = top % LANES, top // LANES
        spans = {t: slice(t * LANES, (t + 1) * LANES) for t in range(tile, W // LANES)}
        rows = [
            {t: jnp.broadcast_to(work[top + k : top + k + 1, span], (8, LANES)) for t, span in spans.items()}
            for k in range(8)
        ]
        head = [
            [None] * i + [jnp.broadcast_to(rows[i][tile][:, at + j : at + j + 1], (8, LANES)) for j in range(i, 8)]
            for i in range(8)
        ]
        inverse = []
        for k in range(8):
            inverse.append(lax.rsqrt(head[k][k]))
            for j in range(k + 1, 8):
                head[k][j] = head[k][j] * inverse[k]
            for t in spans:
                rows[k][t] = rows[k][t] * inverse[k]
            for i in range(k + 1, 8):
                for j in range(i, 8):
                    head[i][j] = head[i][j] - head[k][i] * head[k][j]
                for t in spans:
                    rows[i][t] = rows[i][t] - head[k][i] * rows[k][t]
        for t in range(tile):
            factor[top : top + 8, t * LANES : (t + 1) * LANES] = jnp.zeros((8, LANES), F32)
        for t, span in spans.items():
            value = rows[0][t]
            for k in range(1, 8):
                value = jnp.where(sub == k, rows[k][t], value)
            if t == tile:
                value = jnp.where(lane - at >= sub, value, 0.0)
            factor[top : top + 8, span] = value
        first = top // block * block
        last = first + block
        if top + 8 < last:
            solved = [None] * 8
            for k in reversed(range(8)):
                solved[k] = {}
                for t in spans:
                    value = rows[k][t]
                    for i in range(7, k, -1):
                        value = value - head[k][i] * solved[i][t]
                    solved[k][t] = value * inverse[k]
            for g in range(top + 8, last, 8):
                left = work[g : g + 8, spans[tile]]
                sides = [jnp.broadcast_to(left[:, at + j : at + j + 1], (8, LANES)) for j in range(8)]
                for t, span in spans.items():
                    work[g : g + 8, span] = work[g : g + 8, span] - total([sides[j] * solved[j][t] for j in range(8)])
        elif last < W:
            start = last // LANES * LANES
            done = factor[first:last, start:]
            for a, b in ((last, last + block), (last + block, W)):
                if a < b:
                    work[a:b, start:] = work[a:b, start:] - lax.dot_general(
                        done[:, a - start : b - start],
                        done,
                        (((0,), (0,)), ((), ())),
                        precision=HIGHEST,
                        preferred_element_type=F32,
                    )


def on_device(matrix, signs, picks):
    zh, c = lax.axis_index("zh"), lax.axis_index("core")
    ids = jnp.stack([zh, c]).astype(jnp.int32)
    table = pl.pallas_call(
        local_kernel,
        out_shape=shape(OUTER, W, ORDER),
        in_specs=[VMEM, VMEM],
        out_specs=VMEM,
        compiler_params=params(16),
        name="local",
    )(matrix, signs.reshape(OUTER * 2, LANES))
    packed = pl.pallas_call(
        pack_kernel,
        out_shape=shape(GROUP * CHUNK, LANES),
        in_specs=[VMEM] * 2,
        out_specs=VMEM,
        compiler_params=params(16),
        name="pack",
    )(table, picks.reshape(1, SAMP))
    packed = packed.reshape(GROUP, CHUNK // 2, 2, LANES)
    packed = lax.all_to_all(packed, ("core", "z0", "x", "y"), 0, 0, tiled=True).reshape(GROUP * CHUNK, LANES)

    local = pl.pallas_call(
        picks_kernel,
        out_shape=jax.ShapeDtypeStruct((GROUP, LANES), jnp.int32),
        in_specs=[VMEM],
        out_specs=VMEM,
        compiler_params=params(16),
        name="picks",
    )(packed)
    line = [local] + [lax.ppermute(local, "zh", [(i, i ^ d) for i in range(NZH)]) for d in (1, 2, 3)]
    table = pl.pallas_call(
        transform_kernel,
        out_shape=shape(GROUP * OUTER, 8, LANES),
        in_specs=[VMEM],
        out_specs=VMEM,
        compiler_params=params(16),
        cost_estimate=pl.CostEstimate(flops=10_000_000, bytes_accessed=8_000_000, transcendentals=0),
        name="transform",
    )(packed)
    sampled = pl.pallas_call(
        gather_kernel,
        out_shape=shape(NZH, CHIPS // NZH * COLS, LANES),
        in_specs=[SMEM] + [VMEM] * 5,
        out_specs=VMEM,
        compiler_params=params(16),
        name="gather",
    )(ids, table, *line)
    sampled = lax.all_to_all(
        sampled.reshape(CHIPS, COLS, LANES), ("zh", "z0", "x", "y"), 0, 0, tiled=True
    ).reshape(NZH, CHIPS // NZH * COLS, LANES)

    mine = pl.pallas_call(
        lambda *refs: zsum_kernel(1.0 / math.sqrt(ROWS * 256), *refs),
        out_shape=shape(128, LANES),
        in_specs=[SMEM, VMEM],
        out_specs=VMEM,
        compiler_params=params(4),
        name="zsum",
    )(ids, sampled)
    other = lax.ppermute(mine, "core", [(0, 1), (1, 0)])
    sketch, gram = pl.pallas_call(
        gram_kernel,
        out_shape=[shape(SAMP, W), shape(W // NC, W)],
        in_specs=[SMEM, VMEM, VMEM],
        out_specs=[VMEM, VMEM],
        scratch_shapes=[pltpu.VMEM((W, 128), F32), pltpu.VMEM((128, W), F32)],
        compiler_params=params(4),
        name="gram",
    )(ids, mine, other)

    def spread(blocks, count, scale, name):
        return pl.pallas_call(
            lambda *refs: spread_kernel(scale, *refs),
            out_shape=shape(count, 8, W),
            in_specs=[VMEM],
            out_specs=VMEM,
            compiler_params=params(4),
            name=name,
        )(blocks)

    gram = lax.all_to_all(gram.reshape(NQ, 8, W), ("x", "y"), 0, 0, tiled=True)
    rows = spread(gram, NZ, 1.0, "sum_xy")
    rows = lax.all_to_all(rows, ("zh", "z0"), 0, 0, tiled=True)
    rows = spread(rows, NC * NQ, 1.0 / (SAMP * 256), "sum_z")
    gram = lax.all_to_all(rows, ("core", "x", "y"), 0, 0, tiled=True).reshape(W, W)
    factor = pl.pallas_call(
        factor_kernel,
        out_shape=shape(W, W),
        in_specs=[VMEM],
        out_specs=VMEM,
        scratch_shapes=[pltpu.VMEM((W, W), F32)],
        compiler_params=params(4),
        name="factor",
    )(gram)
    return (sketch, factor)


def solution(mesh):
    devices = mesh.devices.transpose([mesh.axis_names.index(name) for name in ("rows", "grp")])
    split = Mesh(devices.reshape(NX, NZH, NZ0, NC, NY), ("x", "zh", "z0", "core", "y"))
    rows = ("y", "x", "zh", "z0", "core")
    return jax.shard_map(
        on_device,
        mesh=split,
        in_specs=(P(rows, None), P(rows), P(rows)),
        out_specs=(P(rows, None), P()),
        check_vma=False,
    )
```

```python
import math

import jax
import jax.numpy as jnp
from jax import lax
from jax.experimental import pallas as pl
from jax.experimental.pallas import tpu as pltpu
from jax.sharding import Mesh, PartitionSpec as P

NX, NZH, NZ0, NC, NY = 4, 4, 2, 2, 4
NZ = NZH * NZ0
NQ = NX * NY
ROWS = 2048
SAMP = 64
OUTER = 8
ORDER = 256
W = 256
GROUP = NC * NZ0 * NX * NY
COLS = W // GROUP
CHUNK = OUTER * 8 + 2
CHIPS = NZH * NZ0 * NX * NY
LANES = 128
F32 = jnp.float32
HIGHEST = lax.Precision.HIGHEST
VMEM = pl.BlockSpec(memory_space=pltpu.VMEM)
SMEM = pl.BlockSpec(memory_space=pltpu.SMEM)


def params(mib):
    return pltpu.CompilerParams(vmem_limit_bytes=mib * 1024 * 1024)


def shape(*sizes):
    return jax.ShapeDtypeStruct(sizes, F32)


def parity_sign(value):
    return (1 - 2 * ((value ^ (value >> 1)) & 1)).astype(F32)


def butterfly(values):
    values = list(values)
    half = 1
    while half < len(values):
        for first in range(len(values)):
            if first & half == 0:
                a, b = values[first], values[first | half]
                values[first], values[first | half] = a + b, a - b
        half *= 2
    return values


def total(parts):
    while len(parts) > 1:
        parts = [parts[k] + parts[k + 1] for k in range(0, len(parts), 2)]
    return parts[0]


def local_kernel(matrix, signs, table):
    row = lax.broadcasted_iota(jnp.int32, (ORDER, ORDER), 0)
    col = lax.broadcasted_iota(jnp.int32, (ORDER, ORDER), 1)
    both = row & col
    both = both ^ (both >> 4)
    both = both ^ (both >> 2)
    both = both ^ (both >> 1)
    hadamard = (1 - 2 * (both & 1)).astype(F32).astype(jnp.bfloat16)
    for o in range(OUTER):
        block = matrix[o * ORDER : (o + 1) * ORDER, :].astype(F32)
        sign = jnp.concatenate([signs[2 * o : 2 * o + 1, :], signs[2 * o + 1 : 2 * o + 2, :]], axis=1)
        flipped = (block.T * sign.astype(F32)).astype(jnp.bfloat16)
        table[o] = jnp.dot(flipped, hadamard, preferred_element_type=F32)


def pack_kernel(ids, table, p0, p1, p2, p3, out):
    sub = lax.broadcasted_iota(jnp.int32, (8, LANES), 0)
    for o in range(OUTER):
        for pair in range(GROUP // 2):
            low = table[o, pair * 8 : pair * 8 + 8, :LANES]
            high = table[o, pair * 8 : pair * 8 + 8, LANES:]
            spot = 2 * pair * CHUNK + o * 8
            out[spot : spot + 8, :] = jnp.where(sub < 4, low, pltpu.roll(high, 4, 0))
            spot += CHUNK
            out[spot : spot + 8, :] = jnp.where(sub < 4, pltpu.roll(low, 4, 0), high)
    zh = ids[0]
    row = lax.broadcasted_iota(jnp.int32, (2, LANES), 0)
    lane = lax.broadcasted_iota(jnp.int32, (2, LANES), 1)
    tile = jnp.zeros((2, LANES), F32)
    for d, ref in enumerate((p0, p1, p2, p3)):
        place = zh ^ d
        value = (ref[...] & (ROWS - 1)).astype(F32)
        value = jnp.broadcast_to(jnp.concatenate([value, value], axis=1), (2, LANES))
        here = (row == (place >> 1)) & ((lane >> 6) == (place & 1))
        tile = jnp.where(here, value, tile)
    for k in range(GROUP):
        out[k * CHUNK + OUTER * 8 : (k + 1) * CHUNK, :] = tile


def gather_kernel(blocks, out, table):
    for high in range(32):
        values = [blocks[(high * 2 + low) * CHUNK + o * 8 : (high * 2 + low) * CHUNK + o * 8 + 8, :] for low in range(2) for o in range(OUTER)]
        for k, value in enumerate(butterfly(values)):
            table[high * 16 + k] = value
    for rest in range(16):
        values = [table[high * 16 + rest] for high in range(32)]
        for high, value in enumerate(butterfly(values)):
            table[high * 16 + rest] = value
    sub = lax.broadcasted_iota(jnp.int32, (8, LANES), 0)
    lane = lax.broadcasted_iota(jnp.int32, (8, LANES), 1)
    upper, first = sub >= 4, lane < SAMP
    for half in range(GROUP // 4):
        z0, spot = half // (NQ // 2), half % (NQ // 2) * 8
        for zp in range(2):
            rows = []
            for c in range(NC):
                picked = []
                for ylo in range(2):
                    device = (z0 * NC + c) * NQ + spot // 4 + ylo
                    row = device * CHUNK + OUTER * 8 + zp
                    index = blocks[row : row + 1, :].astype(jnp.int32)
                    index = jnp.broadcast_to(index, (8, LANES))
                    low = index & (LANES - 1)
                    level = [
                        jnp.take_along_axis(table[device * 8 + o], low, axis=1, mode="promise_in_bounds")
                        for o in range(OUTER)
                    ]
                    for place in range(3):
                        odd = (index & (ORDER << place)) != 0
                        level = [jnp.where(odd, level[k + 1], level[k]) for k in range(0, len(level), 2)]
                    same = ((index & LANES) != 0) == upper
                    picked.append(jnp.where(same, level[0], pltpu.roll(level[0], 4, 0)))
                rows.append(jnp.where(upper, picked[1], picked[0]))
            turned = [pltpu.roll(row, SAMP, 1) for row in rows]
            out[z0, 2 * zp, spot : spot + 8, :] = jnp.where(first, rows[0], turned[1])
            out[z0, 2 * zp + 1, spot : spot + 8, :] = jnp.where(first, turned[0], rows[1])


def zsum_kernel(scale, ids, blocks, out):
    zh = ids[0]
    for z0 in range(NZ0):
        parts = [blocks[z0, d] * (parity_sign(zh & d) * scale) for d in range(NZH)]
        out[z0 * NQ * COLS : (z0 + 1) * NQ * COLS, :] = total(parts)


def gram_kernel(ids, mine, other, sketch, gram, both, turned):
    c = ids[1]
    part = NQ * COLS
    for z0 in range(NZ0):
        rows = slice(z0 * part, (z0 + 1) * part)
        both[pl.ds(pl.multiple_of((z0 * NC + c) * part, part), part), :] = mine[rows, :]
        both[pl.ds(pl.multiple_of((z0 * NC + 1 - c) * part, part), part), :] = other[rows, :]
    value = both[...]
    turned[...] = value.T
    sketch[...] = turned[pl.ds(pl.multiple_of(c * SAMP, SAMP), SAMP), :]
    half = both[pl.ds(pl.multiple_of(c * 128, 128), 128), :]
    gram[...] = lax.dot_general(
        half, value, (((1,), (1,)), ((), ())), precision=HIGHEST, preferred_element_type=F32
    )


def spread_kernel(scale, blocks, out):
    value = total([blocks[k] for k in range(blocks.shape[0])]) * scale
    for k in range(out.shape[0]):
        out[k] = value


def factor_kernel(gram, factor, work):
    work[...] = gram[...]
    sub = lax.broadcasted_iota(jnp.int32, (8, LANES), 0)
    lane = lax.broadcasted_iota(jnp.int32, (8, LANES), 1)
    block = 32
    for top in range(0, W, 8):
        at, tile = top % LANES, top // LANES
        spans = {t: slice(t * LANES, (t + 1) * LANES) for t in range(tile, W // LANES)}
        rows = [
            {t: jnp.broadcast_to(work[top + k : top + k + 1, span], (8, LANES)) for t, span in spans.items()}
            for k in range(8)
        ]
        head = [
            [None] * i + [jnp.broadcast_to(rows[i][tile][:, at + j : at + j + 1], (8, LANES)) for j in range(i, 8)]
            for i in range(8)
        ]
        inverse = []
        for k in range(8):
            inverse.append(lax.rsqrt(head[k][k]))
            for j in range(k + 1, 8):
                head[k][j] = head[k][j] * inverse[k]
            for t in spans:
                rows[k][t] = rows[k][t] * inverse[k]
            for i in range(k + 1, 8):
                for j in range(i, 8):
                    head[i][j] = head[i][j] - head[k][i] * head[k][j]
                for t in spans:
                    rows[i][t] = rows[i][t] - head[k][i] * rows[k][t]
        for t in range(tile):
            factor[top : top + 8, t * LANES : (t + 1) * LANES] = jnp.zeros((8, LANES), F32)
        for t, span in spans.items():
            value = rows[0][t]
            for k in range(1, 8):
                value = jnp.where(sub == k, rows[k][t], value)
            if t == tile:
                value = jnp.where(lane - at >= sub, value, 0.0)
            factor[top : top + 8, span] = value
        first = top // block * block
        last = first + block
        if top + 8 < last:
            solved = [None] * 8
            for k in reversed(range(8)):
                solved[k] = {}
                for t in spans:
                    value = rows[k][t]
                    for i in range(7, k, -1):
                        value = value - head[k][i] * solved[i][t]
                    solved[k][t] = value * inverse[k]
            for g in range(top + 8, last, 8):
                left = work[g : g + 8, spans[tile]]
                sides = [jnp.broadcast_to(left[:, at + j : at + j + 1], (8, LANES)) for j in range(8)]
                for t, span in spans.items():
                    work[g : g + 8, span] = work[g : g + 8, span] - total([sides[j] * solved[j][t] for j in range(8)])
        elif last < W:
            start = last // LANES * LANES
            done = factor[first:last, start:]
            for a, b in ((last, last + block), (last + block, W)):
                if a < b:
                    work[a:b, start:] = work[a:b, start:] - lax.dot_general(
                        done[:, a - start : b - start],
                        done,
                        (((0,), (0,)), ((), ())),
                        precision=HIGHEST,
                        preferred_element_type=F32,
                    )


def on_device(matrix, signs, picks):
    zh, c = lax.axis_index("zh"), lax.axis_index("core")
    ids = jnp.stack([zh, c]).astype(jnp.int32)
    matrix, ids = lax.optimization_barrier((matrix, ids))
    line = [picks] + [lax.ppermute(picks, "zh", [(i, i ^ d) for i in range(NZH)]) for d in range(1, NZH)]
    line = [value.reshape(1, SAMP) for value in line]

    table = pl.pallas_call(
        local_kernel,
        out_shape=shape(OUTER, W, ORDER),
        in_specs=[VMEM, VMEM],
        out_specs=VMEM,
        compiler_params=params(16),
        name="local",
    )(matrix, signs.reshape(OUTER * 2, LANES))
    packed = pl.pallas_call(
        pack_kernel,
        out_shape=shape(GROUP * CHUNK, LANES),
        in_specs=[SMEM] + [VMEM] * 5,
        out_specs=VMEM,
        compiler_params=params(16),
        name="pack",
    )(ids, table, *line)
    packed = packed.reshape(GROUP, CHUNK // 2, 2, LANES)
    packed = lax.all_to_all(packed, ("z0", "core", "x", "y"), 0, 0, tiled=True).reshape(GROUP * CHUNK, LANES)

    sampled = pl.pallas_call(
        gather_kernel,
        out_shape=shape(NZ0, NZH, NQ * COLS, LANES),
        in_specs=[VMEM],
        out_specs=VMEM,
        scratch_shapes=[pltpu.VMEM((GROUP * OUTER, 8, LANES), F32)],
        compiler_params=params(16),
        name="gather",
    )(packed)
    sampled = lax.all_to_all(
        sampled.reshape(CHIPS, COLS, LANES), ("z0", "zh", "x", "y"), 0, 0, tiled=True
    ).reshape(NZ0, NZH, NQ * COLS, LANES)

    mine = pl.pallas_call(
        lambda *refs: zsum_kernel(1.0 / math.sqrt(ROWS * 256), *refs),
        out_shape=shape(128, LANES),
        in_specs=[SMEM, VMEM],
        out_specs=VMEM,
        compiler_params=params(4),
        name="zsum",
    )(ids, sampled)
    other = lax.ppermute(mine, "core", [(0, 1), (1, 0)])
    sketch, gram = pl.pallas_call(
        gram_kernel,
        out_shape=[shape(SAMP, W), shape(W // NC, W)],
        in_specs=[SMEM, VMEM, VMEM],
        out_specs=[VMEM, VMEM],
        scratch_shapes=[pltpu.VMEM((W, 128), F32), pltpu.VMEM((128, W), F32)],
        compiler_params=params(4),
        name="gram",
    )(ids, mine, other)

    def spread(blocks, count, scale, name):
        return pl.pallas_call(
            lambda *refs: spread_kernel(scale, *refs),
            out_shape=shape(count, 8, W),
            in_specs=[VMEM],
            out_specs=VMEM,
            compiler_params=params(4),
            name=name,
        )(blocks)

    gram = lax.all_to_all(gram.reshape(NQ, 8, W), ("x", "y"), 0, 0, tiled=True)
    rows = spread(gram, NZ, 1.0, "sum_xy")
    rows = lax.all_to_all(rows, ("zh", "z0"), 0, 0, tiled=True)
    rows = spread(rows, NC * NQ, 1.0 / (SAMP * 256), "sum_z")
    gram = lax.all_to_all(rows, ("core", "x", "y"), 0, 0, tiled=True).reshape(W, W)
    factor = pl.pallas_call(
        factor_kernel,
        out_shape=shape(W, W),
        in_specs=[VMEM],
        out_specs=VMEM,
        scratch_shapes=[pltpu.VMEM((W, W), F32)],
        compiler_params=params(4),
        name="factor",
    )(gram)
    return (sketch, factor)


def solution(mesh):
    devices = mesh.devices.transpose([mesh.axis_names.index(name) for name in ("rows", "grp")])
    split = Mesh(devices.reshape(NX, NZH, NZ0, NC, NY), ("x", "zh", "z0", "core", "y"))
    rows = ("y", "x", "zh", "z0", "core")
    return jax.shard_map(
        on_device,
        mesh=split,
        in_specs=(P(rows, None), P(rows), P(rows)),
        out_specs=(P(rows, None), P()),
        check_vma=False,
    )
```

```python
import math

import jax
import jax.numpy as jnp
from jax import lax
from jax.experimental import pallas as pl
from jax.experimental.pallas import tpu as pltpu
from jax.sharding import Mesh, PartitionSpec as P

NX, NZH, NZ0, NC, NY = 4, 4, 2, 2, 4
NZ = NZH * NZ0
NQ = NX * NY
ROWS = 2048
SAMP = 64
OUTER = 8
ORDER = 256
W = 256
GROUP = NC * NZ0 * NX * NY
COLS = W // GROUP
CHUNK = OUTER * 8 + 2
CHIPS = NZH * NZ0 * NX * NY
LANES = 128
LINE = (0, 2, 1, 3)
F32 = jnp.float32
HIGHEST = lax.Precision.HIGHEST
VMEM = pl.BlockSpec(memory_space=pltpu.VMEM)
SMEM = pl.BlockSpec(memory_space=pltpu.SMEM)


def params(mib):
    return pltpu.CompilerParams(vmem_limit_bytes=mib * 1024 * 1024)


def shape(*sizes):
    return jax.ShapeDtypeStruct(sizes, F32)


def parity_sign(value):
    return (1 - 2 * ((value ^ (value >> 1)) & 1)).astype(F32)


def butterfly(values):
    values = list(values)
    half = 1
    while half < len(values):
        for first in range(len(values)):
            if first & half == 0:
                a, b = values[first], values[first | half]
                values[first], values[first | half] = a + b, a - b
        half *= 2
    return values


def total(parts):
    while len(parts) > 1:
        parts = [parts[k] + parts[k + 1] for k in range(0, len(parts), 2)]
    return parts[0]


def local_kernel(matrix, signs, table):
    row = lax.broadcasted_iota(jnp.int32, (ORDER, ORDER), 0)
    col = lax.broadcasted_iota(jnp.int32, (ORDER, ORDER), 1)
    both = row & col
    both = both ^ (both >> 4)
    both = both ^ (both >> 2)
    both = both ^ (both >> 1)
    hadamard = (1 - 2 * (both & 1)).astype(F32).astype(jnp.bfloat16)
    for o in range(OUTER):
        block = matrix[o * ORDER : (o + 1) * ORDER, :].astype(F32)
        sign = jnp.concatenate([signs[2 * o : 2 * o + 1, :], signs[2 * o + 1 : 2 * o + 2, :]], axis=1)
        flipped = (block.T * sign.astype(F32)).astype(jnp.bfloat16)
        table[o] = jnp.dot(flipped, hadamard, preferred_element_type=F32)


def pack_kernel(ids, table, p0, p1, p2, p3, out):
    sub = lax.broadcasted_iota(jnp.int32, (8, LANES), 0)
    for o in range(OUTER):
        for pair in range(GROUP // 2):
            low = table[o, pair * 8 : pair * 8 + 8, :LANES]
            high = table[o, pair * 8 : pair * 8 + 8, LANES:]
            spot = 2 * pair * CHUNK + o * 8
            out[spot : spot + 8, :] = jnp.where(sub < 4, low, pltpu.roll(high, 4, 0))
            spot += CHUNK
            out[spot : spot + 8, :] = jnp.where(sub < 4, pltpu.roll(low, 4, 0), high)
    zh, c = ids[0], ids[1]
    row = lax.broadcasted_iota(jnp.int32, (2, LANES), 0)
    lane = lax.broadcasted_iota(jnp.int32, (2, LANES), 1)
    tile = jnp.zeros((2, LANES), F32)
    for d, ref in zip(LINE, (p0, p1, p2, p3)):
        place = zh ^ d
        value = (ref[...] & (ROWS - 1)).astype(F32)
        value = jnp.broadcast_to(jnp.concatenate([value, value], axis=1), (2, LANES))
        here = (row == (place >> 1)) & ((lane >> 6) == ((place & 1) ^ c))
        tile = jnp.where(here, value, tile)
    for k in range(GROUP):
        out[k * CHUNK + OUTER * 8 : (k + 1) * CHUNK, :] = tile


def gather_kernel(blocks, out, table):
    for high in range(32):
        values = [blocks[(high * 2 + low) * CHUNK + o * 8 : (high * 2 + low) * CHUNK + o * 8 + 8, :] for low in range(2) for o in range(OUTER)]
        for k, value in enumerate(butterfly(values)):
            table[high * 16 + k] = value
    for rest in range(16):
        values = [table[high * 16 + rest] for high in range(32)]
        for high, value in enumerate(butterfly(values)):
            table[high * 16 + rest] = value
    sub = lax.broadcasted_iota(jnp.int32, (8, LANES), 0)
    lane = lax.broadcasted_iota(jnp.int32, (8, LANES), 1)
    upper, first = sub >= 4, lane < SAMP
    for half in range(GROUP // 4):
        z0, spot = half // (NQ // 2), half % (NQ // 2) * 8
        for zp in range(2):
            rows = []
            for c in range(NC):
                picked = []
                for ylo in range(2):
                    device = (z0 * NC + c) * NQ + spot // 4 + ylo
                    row = device * CHUNK + OUTER * 8 + zp
                    index = blocks[row : row + 1, :].astype(jnp.int32)
                    index = jnp.broadcast_to(index, (8, LANES))
                    low = index & (LANES - 1)
                    level = [
                        jnp.take_along_axis(table[device * 8 + o], low, axis=1, mode="promise_in_bounds")
                        for o in range(OUTER)
                    ]
                    for place in range(3):
                        odd = (index & (ORDER << place)) != 0
                        level = [jnp.where(odd, level[k + 1], level[k]) for k in range(0, len(level), 2)]
                    same = ((index & LANES) != 0) == upper
                    picked.append(jnp.where(same, level[0], pltpu.roll(level[0], 4, 0)))
                rows.append(jnp.where(upper, picked[1], picked[0]))
            out[z0, 2 * zp, spot : spot + 8, :] = jnp.where(first, rows[0], rows[1])
            out[z0, 2 * zp + 1, spot : spot + 8, :] = jnp.where(first, rows[1], rows[0])


def zsum_kernel(scale, ids, blocks, out):
    zh = ids[0]
    for z0 in range(NZ0):
        parts = [blocks[z0, d] * (parity_sign(zh & d) * scale) for d in range(NZH)]
        value = total(parts)
        value = jnp.where((zh & 1) == 1, pltpu.roll(value, SAMP, 1), value)
        out[z0 * NQ * COLS : (z0 + 1) * NQ * COLS, :] = value


def gram_kernel(ids, mine, other, sketch, gram, both, turned):
    c = ids[1]
    part = NQ * COLS
    for z0 in range(NZ0):
        rows = slice(z0 * part, (z0 + 1) * part)
        both[pl.ds(pl.multiple_of((z0 * NC + c) * part, part), part), :] = mine[rows, :]
        both[pl.ds(pl.multiple_of((z0 * NC + 1 - c) * part, part), part), :] = other[rows, :]
    value = both[...]
    turned[...] = value.T
    sketch[...] = turned[pl.ds(pl.multiple_of(c * SAMP, SAMP), SAMP), :]
    half = both[pl.ds(pl.multiple_of(c * 128, 128), 128), :]
    gram[...] = lax.dot_general(
        half, value, (((1,), (1,)), ((), ())), precision=HIGHEST, preferred_element_type=F32
    )


def spread_kernel(scale, blocks, out):
    value = total([blocks[k] for k in range(blocks.shape[0])]) * scale
    for k in range(out.shape[0]):
        out[k] = value


def factor_kernel(gram, factor, work):
    work[...] = gram[...]
    sub = lax.broadcasted_iota(jnp.int32, (8, LANES), 0)
    lane = lax.broadcasted_iota(jnp.int32, (8, LANES), 1)
    block = 32
    for top in range(0, W, 8):
        at, tile = top % LANES, top // LANES
        spans = {t: slice(t * LANES, (t + 1) * LANES) for t in range(tile, W // LANES)}
        rows = [
            {t: jnp.broadcast_to(work[top + k : top + k + 1, span], (8, LANES)) for t, span in spans.items()}
            for k in range(8)
        ]
        head = [
            [None] * i + [jnp.broadcast_to(rows[i][tile][:, at + j : at + j + 1], (8, LANES)) for j in range(i, 8)]
            for i in range(8)
        ]
        inverse = []
        for k in range(8):
            inverse.append(lax.rsqrt(head[k][k]))
            for j in range(k + 1, 8):
                head[k][j] = head[k][j] * inverse[k]
            for t in spans:
                rows[k][t] = rows[k][t] * inverse[k]
            for i in range(k + 1, 8):
                for j in range(i, 8):
                    head[i][j] = head[i][j] - head[k][i] * head[k][j]
                for t in spans:
                    rows[i][t] = rows[i][t] - head[k][i] * rows[k][t]
        for t in range(tile):
            factor[top : top + 8, t * LANES : (t + 1) * LANES] = jnp.zeros((8, LANES), F32)
        for t, span in spans.items():
            value = rows[0][t]
            for k in range(1, 8):
                value = jnp.where(sub == k, rows[k][t], value)
            if t == tile:
                value = jnp.where(lane - at >= sub, value, 0.0)
            factor[top : top + 8, span] = value
        first = top // block * block
        last = first + block
        if top + 8 < last:
            for g in range(top + 8, last, 8):
                left = work[g : g + 8, spans[tile]]
                sides = [jnp.broadcast_to(left[:, at + j : at + j + 1], (8, LANES)) for j in range(8)]
                for k in range(8):
                    sides[k] = sides[k] * inverse[k]
                    for j in range(k + 1, 8):
                        sides[j] = sides[j] - sides[k] * head[k][j]
                for t, span in spans.items():
                    work[g : g + 8, span] = work[g : g + 8, span] - total([sides[k] * rows[k][t] for k in range(8)])
        elif last < W:
            start = last // LANES * LANES
            done = factor[first:last, start:]
            for a, b in ((last, last + block), (last + block, W)):
                if a < b:
                    work[a:b, start:] = work[a:b, start:] - lax.dot_general(
                        done[:, a - start : b - start],
                        done,
                        (((0,), (0,)), ((), ())),
                        precision=HIGHEST,
                        preferred_element_type=F32,
                    )


def on_device(matrix, signs, picks):
    zh, c = lax.axis_index("zh"), lax.axis_index("core")
    ids = jnp.stack([zh, c]).astype(jnp.int32)
    matrix, ids = lax.optimization_barrier((matrix, ids))
    line = [picks] + [lax.ppermute(picks, "zh", [(i, i ^ d) for i in range(NZH)]) for d in range(1, NZH)]
    line = [value.reshape(1, SAMP) for value in line]

    table = pl.pallas_call(
        local_kernel,
        out_shape=shape(OUTER, W, ORDER),
        in_specs=[VMEM, VMEM],
        out_specs=VMEM,
        compiler_params=params(16),
        name="local",
    )(matrix, signs.reshape(OUTER * 2, LANES))
    packed = pl.pallas_call(
        pack_kernel,
        out_shape=shape(GROUP * CHUNK, LANES),
        in_specs=[SMEM] + [VMEM] * 5,
        out_specs=VMEM,
        compiler_params=params(16),
        name="pack",
    )(ids, table, *[line[d] for d in LINE])
    packed = packed.reshape(GROUP, CHUNK // 2, 2, LANES)
    packed = lax.all_to_all(packed, ("z0", "core", "x", "y"), 0, 0, tiled=True).reshape(GROUP * CHUNK, LANES)

    sampled = pl.pallas_call(
        gather_kernel,
        out_shape=shape(NZ0, NZH, NQ * COLS, LANES),
        in_specs=[VMEM],
        out_specs=VMEM,
        scratch_shapes=[pltpu.VMEM((GROUP * OUTER, 8, LANES), F32)],
        compiler_params=params(16),
        name="gather",
    )(packed)
    sampled = lax.all_to_all(
        sampled.reshape(CHIPS, COLS, LANES), ("z0", "zh", "x", "y"), 0, 0, tiled=True
    ).reshape(NZ0, NZH, NQ * COLS, LANES)

    mine = pl.pallas_call(
        lambda *refs: zsum_kernel(1.0 / math.sqrt(ROWS * 256), *refs),
        out_shape=shape(128, LANES),
        in_specs=[SMEM, VMEM],
        out_specs=VMEM,
        compiler_params=params(4),
        name="zsum",
    )(ids, sampled)
    other = lax.ppermute(mine, "core", [(0, 1), (1, 0)])
    sketch, gram = pl.pallas_call(
        gram_kernel,
        out_shape=[shape(SAMP, W), shape(W // NC, W)],
        in_specs=[SMEM, VMEM, VMEM],
        out_specs=[VMEM, VMEM],
        scratch_shapes=[pltpu.VMEM((W, 128), F32), pltpu.VMEM((128, W), F32)],
        compiler_params=params(4),
        name="gram",
    )(ids, mine, other)

    def spread(blocks, count, scale, name):
        return pl.pallas_call(
            lambda *refs: spread_kernel(scale, *refs),
            out_shape=shape(count, 8, W),
            in_specs=[VMEM],
            out_specs=VMEM,
            compiler_params=params(4),
            name=name,
        )(blocks)

    gram = lax.all_to_all(gram.reshape(NQ, 8, W), ("x", "y"), 0, 0, tiled=True)
    rows = spread(gram, NZ, 1.0, "sum_xy")
    rows = lax.all_to_all(rows, ("zh", "z0"), 0, 0, tiled=True)
    rows = spread(rows, NC * NQ, 1.0 / (SAMP * 256), "sum_z")
    gram = lax.all_to_all(rows, ("core", "x", "y"), 0, 0, tiled=True).reshape(W, W)
    factor = pl.pallas_call(
        factor_kernel,
        out_shape=shape(W, W),
        in_specs=[VMEM],
        out_specs=VMEM,
        scratch_shapes=[pltpu.VMEM((W, W), F32)],
        compiler_params=params(4),
        name="factor",
    )(gram)
    return (sketch, factor)


def solution(mesh):
    devices = mesh.devices.transpose([mesh.axis_names.index(name) for name in ("rows", "grp")])
    split = Mesh(devices.reshape(NX, NZH, NZ0, NC, NY), ("x", "zh", "z0", "core", "y"))
    rows = ("y", "x", "zh", "z0", "core")
    return jax.shard_map(
        on_device,
        mesh=split,
        in_specs=(P(rows, None), P(rows), P(rows)),
        out_specs=(P(rows, None), P()),
        check_vma=False,
    )
```

```python
import math

import jax
import jax.numpy as jnp
from jax import lax
from jax.experimental import pallas as pl
from jax.experimental.pallas import tpu as pltpu
from jax.sharding import Mesh, PartitionSpec as P

NX, NZH, NZ0, NC, NY = 4, 4, 2, 2, 4
NZ = NZH * NZ0
NQ = NX * NY
ROWS = 2048
SAMP = 64
OUTER = 8
ORDER = 256
W = 256
GROUP = NC * NZ0 * NX * NY
COLS = W // GROUP
CHUNK = OUTER * 8 + 2
CHIPS = NZH * NZ0 * NX * NY
LANES = 128
LINE = (0, 2, 1, 3)
F32 = jnp.float32
HIGHEST = lax.Precision.HIGHEST
VMEM = pl.BlockSpec(memory_space=pltpu.VMEM)


def params(mib):
    return pltpu.CompilerParams(vmem_limit_bytes=mib * 1024 * 1024)


def shape(*sizes):
    return jax.ShapeDtypeStruct(sizes, F32)


def parity_sign(value):
    return (1 - 2 * ((value ^ (value >> 1)) & 1)).astype(F32)


def butterfly(values):
    values = list(values)
    half = 1
    while half < len(values):
        for first in range(len(values)):
            if first & half == 0:
                a, b = values[first], values[first | half]
                values[first], values[first | half] = a + b, a - b
        half *= 2
    return values


def total(parts):
    while len(parts) > 1:
        parts = [parts[k] + parts[k + 1] for k in range(0, len(parts), 2)]
    return parts[0]


def local_kernel(matrix, signs, table):
    row = lax.broadcasted_iota(jnp.int32, (ORDER, ORDER), 0)
    col = lax.broadcasted_iota(jnp.int32, (ORDER, ORDER), 1)
    both = row & col
    both = both ^ (both >> 4)
    both = both ^ (both >> 2)
    both = both ^ (both >> 1)
    hadamard = (1 - 2 * (both & 1)).astype(F32).astype(jnp.bfloat16)
    for o in range(OUTER):
        block = matrix[o * ORDER : (o + 1) * ORDER, :].astype(F32)
        sign = jnp.concatenate([signs[2 * o : 2 * o + 1, :], signs[2 * o + 1 : 2 * o + 2, :]], axis=1)
        flipped = (block.T * sign.astype(F32)).astype(jnp.bfloat16)
        table[o] = jnp.dot(flipped, hadamard, preferred_element_type=F32)


def pack_kernel(ids, table, p0, p1, p2, p3, out):
    sub = lax.broadcasted_iota(jnp.int32, (8, LANES), 0)
    for o in range(OUTER):
        for pair in range(GROUP // 2):
            low = table[o, pair * 8 : pair * 8 + 8, :LANES]
            high = table[o, pair * 8 : pair * 8 + 8, LANES:]
            spot = 2 * pair * CHUNK + o * 8
            out[spot : spot + 8, :] = jnp.where(sub < 4, low, pltpu.roll(high, 4, 0))
            spot += CHUNK
            out[spot : spot + 8, :] = jnp.where(sub < 4, pltpu.roll(low, 4, 0), high)
    zh, c = ids[0:1, :], ids[1:2, :]
    row = lax.broadcasted_iota(jnp.int32, (2, LANES), 0)
    lane = lax.broadcasted_iota(jnp.int32, (2, LANES), 1)
    tile = jnp.zeros((2, LANES), F32)
    for d, ref in zip(LINE, (p0, p1, p2, p3)):
        place = zh ^ d
        value = (ref[...] & (ROWS - 1)).astype(F32)
        value = jnp.broadcast_to(jnp.concatenate([value, value], axis=1), (2, LANES))
        here = (row == (place >> 1)) & ((lane >> 6) == ((place & 1) ^ c))
        tile = jnp.where(here, value, tile)
    for k in range(GROUP):
        out[k * CHUNK + OUTER * 8 : (k + 1) * CHUNK, :] = tile


def gather_kernel(blocks, out, table):
    for high in range(32):
        values = [blocks[(high * 2 + low) * CHUNK + o * 8 : (high * 2 + low) * CHUNK + o * 8 + 8, :] for low in range(2) for o in range(OUTER)]
        for k, value in enumerate(butterfly(values)):
            table[high * 16 + k] = value
    for rest in range(16):
        values = [table[high * 16 + rest] for high in range(32)]
        for high, value in enumerate(butterfly(values)):
            table[high * 16 + rest] = value
    sub = lax.broadcasted_iota(jnp.int32, (8, LANES), 0)
    lane = lax.broadcasted_iota(jnp.int32, (8, LANES), 1)
    upper, first = sub >= 4, lane < SAMP
    for half in range(GROUP // 4):
        z0, spot = half // (NQ // 2), half % (NQ // 2) * 8
        for zp in range(2):
            rows = []
            for c in range(NC):
                picked = []
                for ylo in range(2):
                    device = (z0 * NC + c) * NQ + spot // 4 + ylo
                    row = device * CHUNK + OUTER * 8 + zp
                    index = blocks[row : row + 1, :].astype(jnp.int32)
                    index = jnp.broadcast_to(index, (8, LANES))
                    low = index & (LANES - 1)
                    level = [
                        jnp.take_along_axis(table[device * 8 + o], low, axis=1, mode="promise_in_bounds")
                        for o in range(OUTER)
                    ]
                    for place in range(3):
                        odd = (index & (ORDER << place)) != 0
                        level = [jnp.where(odd, level[k + 1], level[k]) for k in range(0, len(level), 2)]
                    same = ((index & LANES) != 0) == upper
                    picked.append(jnp.where(same, level[0], pltpu.roll(level[0], 4, 0)))
                rows.append(jnp.where(upper, picked[1], picked[0]))
            out[z0, 2 * zp, spot : spot + 8, :] = jnp.where(first, rows[0], rows[1])
            out[z0, 2 * zp + 1, spot : spot + 8, :] = jnp.where(first, rows[1], rows[0])


def zsum_kernel(scale, ids, blocks, out):
    zh = ids[0:1, :]
    odd = jnp.broadcast_to(zh, (8, LANES)) & 1 == 1
    signs = [jnp.broadcast_to(parity_sign(zh & d) * scale, (8, LANES)) for d in range(NZH)]
    for z0 in range(NZ0):
        for spot in range(0, NQ * COLS, 8):
            value = total([blocks[z0, d, spot : spot + 8, :] * signs[d] for d in range(NZH)])
            value = jnp.where(odd, pltpu.roll(value, SAMP, 1), value)
            out[z0 * NQ * COLS + spot : z0 * NQ * COLS + spot + 8, :] = value


def gram_kernel(ids, mine, other, sketch, gram):
    part = NQ * COLS
    zero = jnp.broadcast_to(ids[1:2, :], (part, LANES)) == 0
    pieces = []
    for z0 in range(NZ0):
        a, b = mine[z0 * part : (z0 + 1) * part, :], other[z0 * part : (z0 + 1) * part, :]
        pieces += [jnp.where(zero, a, b), jnp.where(zero, b, a)]
    low, high = jnp.concatenate(pieces[:2], axis=0), jnp.concatenate(pieces[2:], axis=0)
    value = jnp.concatenate([low, high], axis=0)
    zero = jnp.broadcast_to(ids[1:2, :], (W // NC, LANES)) == 0
    gram[...] = lax.dot_general(
        jnp.where(zero, low, high), value, (((1,), (1,)), ((), ())), precision=HIGHEST, preferred_element_type=F32
    )
    for tile, block in enumerate((low, high)):
        turned = block.T
        sketch[:, tile * LANES : (tile + 1) * LANES] = jnp.where(zero[:SAMP], turned[:SAMP], turned[SAMP:])


def spread_kernel(scale, blocks, out):
    value = total([blocks[k] for k in range(blocks.shape[0])]) * scale
    for k in range(out.shape[0]):
        out[k] = value


def factor_kernel(gram, rows_in, factor, rows_out, work):
    rows_out[...] = rows_in[...]
    work[...] = gram[...]
    sub = lax.broadcasted_iota(jnp.int32, (8, LANES), 0)
    lane = lax.broadcasted_iota(jnp.int32, (8, LANES), 1)
    block = 64
    for top in range(0, W, 8):
        at, tile = top % LANES, top // LANES
        spans = {t: slice(t * LANES, (t + 1) * LANES) for t in range(tile, W // LANES)}
        rows = [
            {t: jnp.broadcast_to(work[top + k : top + k + 1, span], (8, LANES)) for t, span in spans.items()}
            for k in range(8)
        ]
        head = [
            [None] * i + [jnp.broadcast_to(rows[i][tile][:, at + j : at + j + 1], (8, LANES)) for j in range(i, 8)]
            for i in range(8)
        ]
        inverse = []
        for k in range(8):
            inverse.append(lax.rsqrt(head[k][k]))
            for j in range(k + 1, 8):
                head[k][j] = head[k][j] * inverse[k]
            for t in spans:
                rows[k][t] = rows[k][t] * inverse[k]
            for i in range(k + 1, 8):
                for j in range(i, 8):
                    head[i][j] = head[i][j] - head[k][i] * head[k][j]
                for t in spans:
                    rows[i][t] = rows[i][t] - head[k][i] * rows[k][t]
        for t in range(tile):
            factor[top : top + 8, t * LANES : (t + 1) * LANES] = jnp.zeros((8, LANES), F32)
        for t, span in spans.items():
            value = rows[0][t]
            for k in range(1, 8):
                value = jnp.where(sub == k, rows[k][t], value)
            if t == tile:
                value = jnp.where(lane - at >= sub, value, 0.0)
            factor[top : top + 8, span] = value
        first = top // block * block
        last = first + block
        if top + 8 < last:
            for g in range(top + 8, last, 8):
                left = work[g : g + 8, spans[tile]]
                sides = [jnp.broadcast_to(left[:, at + j : at + j + 1], (8, LANES)) for j in range(8)]
                for k in range(8):
                    sides[k] = sides[k] * inverse[k]
                    for j in range(k + 1, 8):
                        sides[j] = sides[j] - sides[k] * head[k][j]
                for t, span in spans.items():
                    work[g : g + 8, span] = work[g : g + 8, span] - total([sides[k] * rows[k][t] for k in range(8)])
        elif last < W:
            start = last // LANES * LANES
            done = factor[first:last, start:]
            for a, b in ((last, last + block), (last + block, W)):
                if a < b:
                    work[a:b, start:] = work[a:b, start:] - lax.dot_general(
                        done[:, a - start : b - start],
                        done,
                        (((0,), (0,)), ((), ())),
                        precision=HIGHEST,
                        preferred_element_type=F32,
                    )


def on_device(matrix, signs, picks):
    zh, c = lax.axis_index("zh"), lax.axis_index("core")
    ids = jnp.broadcast_to(jnp.stack([zh, c]).astype(jnp.int32)[:, None], (2, LANES))
    matrix, ids = lax.optimization_barrier((matrix, ids))
    line = [picks] + [lax.ppermute(picks, "zh", [(i, i ^ d) for i in range(NZH)]) for d in range(1, NZH)]
    line = [value.reshape(1, SAMP) for value in line]

    table = pl.pallas_call(
        local_kernel,
        out_shape=shape(OUTER, W, ORDER),
        in_specs=[VMEM, VMEM],
        out_specs=VMEM,
        compiler_params=params(16),
        name="local",
    )(matrix, signs.reshape(OUTER * 2, LANES))
    packed = pl.pallas_call(
        pack_kernel,
        out_shape=shape(GROUP * CHUNK, LANES),
        in_specs=[VMEM] * 6,
        out_specs=VMEM,
        compiler_params=params(16),
        name="pack",
    )(ids, table, *[line[d] for d in LINE])
    packed = packed.reshape(GROUP, CHUNK // 2, 2, LANES)
    packed = lax.all_to_all(packed, ("z0", "core", "x", "y"), 0, 0, tiled=True).reshape(GROUP * CHUNK, LANES)

    sampled = pl.pallas_call(
        gather_kernel,
        out_shape=shape(NZ0, NZH, NQ * COLS, LANES),
        in_specs=[VMEM],
        out_specs=VMEM,
        scratch_shapes=[pltpu.VMEM((GROUP * OUTER, 8, LANES), F32)],
        compiler_params=params(16),
        name="gather",
    )(packed)
    sampled = lax.all_to_all(
        sampled.reshape(CHIPS, COLS, LANES), ("z0", "zh", "x", "y"), 0, 0, tiled=True
    ).reshape(NZ0, NZH, NQ * COLS, LANES)

    mine = pl.pallas_call(
        lambda *refs: zsum_kernel(1.0 / math.sqrt(ROWS * 256), *refs),
        out_shape=shape(128, LANES),
        in_specs=[VMEM, VMEM],
        out_specs=VMEM,
        compiler_params=params(4),
        name="zsum",
    )(ids, sampled)
    other = lax.ppermute(mine, "core", [(0, 1), (1, 0)])
    sketch, gram = pl.pallas_call(
        gram_kernel,
        out_shape=[shape(SAMP, W), shape(W // NC, W)],
        in_specs=[VMEM, VMEM, VMEM],
        out_specs=[VMEM, VMEM],
        compiler_params=params(4),
        name="gram",
    )(ids, mine, other)

    def spread(blocks, count, scale, name):
        return pl.pallas_call(
            lambda *refs: spread_kernel(scale, *refs),
            out_shape=shape(count, 8, W),
            in_specs=[VMEM],
            out_specs=VMEM,
            compiler_params=params(4),
            name=name,
        )(blocks)

    gram = lax.all_to_all(gram.reshape(NQ, 8, W), ("x", "y"), 0, 0, tiled=True)
    rows = spread(gram, NZ, 1.0, "sum_xy")
    rows = lax.all_to_all(rows, ("zh", "z0"), 0, 0, tiled=True)
    rows = spread(rows, NC * NQ, 1.0 / (SAMP * 256), "sum_z")
    gram = lax.all_to_all(rows, ("core", "x", "y"), 0, 0, tiled=True).reshape(W, W)
    factor, sketch = pl.pallas_call(
        factor_kernel,
        out_shape=[shape(W, W), shape(SAMP, W)],
        in_specs=[VMEM, VMEM],
        out_specs=[VMEM, VMEM],
        scratch_shapes=[pltpu.VMEM((W, W), F32)],
        compiler_params=params(4),
        name="factor",
    )(gram, sketch)
    return (sketch, factor)


def solution(mesh):
    devices = mesh.devices.transpose([mesh.axis_names.index(name) for name in ("rows", "grp")])
    split = Mesh(devices.reshape(NX, NZH, NZ0, NC, NY), ("x", "zh", "z0", "core", "y"))
    rows = ("y", "x", "zh", "z0", "core")
    return jax.shard_map(
        on_device,
        mesh=split,
        in_specs=(P(rows, None), P(rows), P(rows)),
        out_specs=(P(rows, None), P()),
        check_vma=False,
    )
```

```python
import math

import jax
import jax.numpy as jnp
from jax import lax
from jax.experimental import pallas as pl
from jax.experimental.pallas import tpu as pltpu
from jax.sharding import Mesh, PartitionSpec as P

NX, NZH, NZ0, NC, NY = 4, 4, 2, 2, 4
NZ = NZH * NZ0
NQ = NX * NY
ROWS = 2048
SAMP = 64
OUTER = 8
ORDER = 256
W = 256
GROUP = NC * NZ0 * NX * NY
COLS = W // GROUP
CHUNK = OUTER * 8 + 2
CHIPS = NZH * NZ0 * NX * NY
LANES = 128
LINE = (0, 2, 1, 3)
F32 = jnp.float32
HIGHEST = lax.Precision.HIGHEST
VMEM = pl.BlockSpec(memory_space=pltpu.VMEM)


def params(mib):
    return pltpu.CompilerParams(vmem_limit_bytes=mib * 1024 * 1024)


def shape(*sizes):
    return jax.ShapeDtypeStruct(sizes, F32)


def parity_sign(value):
    return (1 - 2 * ((value ^ (value >> 1)) & 1)).astype(F32)


def butterfly(values):
    values = list(values)
    half = 1
    while half < len(values):
        for first in range(len(values)):
            if first & half == 0:
                a, b = values[first], values[first | half]
                values[first], values[first | half] = a + b, a - b
        half *= 2
    return values


def total(parts):
    while len(parts) > 1:
        parts = [parts[k] + parts[k + 1] for k in range(0, len(parts), 2)]
    return parts[0]


def local_kernel(matrix, signs, table):
    row = lax.broadcasted_iota(jnp.int32, (ORDER, ORDER), 0)
    col = lax.broadcasted_iota(jnp.int32, (ORDER, ORDER), 1)
    both = row & col
    both = both ^ (both >> 4)
    both = both ^ (both >> 2)
    both = both ^ (both >> 1)
    hadamard = (1 - 2 * (both & 1)).astype(F32).astype(jnp.bfloat16)
    for o in range(OUTER):
        block = matrix[o * ORDER : (o + 1) * ORDER, :].astype(F32)
        sign = jnp.concatenate([signs[2 * o : 2 * o + 1, :], signs[2 * o + 1 : 2 * o + 2, :]], axis=1)
        flipped = (block.T * sign.astype(F32)).astype(jnp.bfloat16)
        table[o] = jnp.dot(flipped, hadamard, preferred_element_type=F32)


def pack_kernel(ids, table, p0, p1, p2, p3, out):
    sub = lax.broadcasted_iota(jnp.int32, (8, LANES), 0)
    for o in range(OUTER):
        for pair in range(GROUP // 2):
            low = table[o, pair * 8 : pair * 8 + 8, :LANES]
            high = table[o, pair * 8 : pair * 8 + 8, LANES:]
            spot = 2 * pair * CHUNK + o * 8
            out[spot : spot + 8, :] = jnp.where(sub < 4, low, pltpu.roll(high, 4, 0))
            spot += CHUNK
            out[spot : spot + 8, :] = jnp.where(sub < 4, pltpu.roll(low, 4, 0), high)
    zh, c = ids[0:1, :], ids[1:2, :]
    row = lax.broadcasted_iota(jnp.int32, (2, LANES), 0)
    lane = lax.broadcasted_iota(jnp.int32, (2, LANES), 1)
    tile = jnp.zeros((2, LANES), F32)
    for d, ref in zip(LINE, (p0, p1, p2, p3)):
        place = zh ^ d
        value = (ref[...] & (ROWS - 1)).astype(F32)
        value = jnp.broadcast_to(jnp.concatenate([value, value], axis=1), (2, LANES))
        here = (row == (place >> 1)) & ((lane >> 6) == ((place & 1) ^ c))
        tile = jnp.where(here, value, tile)
    for k in range(GROUP):
        out[k * CHUNK + OUTER * 8 : (k + 1) * CHUNK, :] = tile


def gather_kernel(ids, blocks, out, table):
    for high in range(32):
        values = [blocks[(high * 2 + low) * CHUNK + o * 8 : (high * 2 + low) * CHUNK + o * 8 + 8, :] for low in range(2) for o in range(OUTER)]
        for k, value in enumerate(butterfly(values)):
            table[high * 16 + k] = value
    for rest in range(16):
        values = [table[high * 16 + rest] for high in range(32)]
        for high, value in enumerate(butterfly(values)):
            table[high * 16 + rest] = value
    sub = lax.broadcasted_iota(jnp.int32, (8, LANES), 0)
    lane = lax.broadcasted_iota(jnp.int32, (8, LANES), 1)
    upper, first = sub >= 4, lane < SAMP
    zh, half_lane = ids[0:1, :], lane[0:1, :] >> 6
    far = [[((zh >> 1) != zp) & (half_lane == ((zh & 1) ^ c)) for c in range(NC)] for zp in range(2)]
    for half in range(GROUP // 4):
        z0, spot = half // (NQ // 2), half % (NQ // 2) * 8
        for zp in range(2):
            rows = []
            for c in range(NC):
                picked = []
                for ylo in range(2):
                    device = (z0 * NC + c) * NQ + spot // 4 + ylo
                    row = device * CHUNK + OUTER * 8 + zp
                    cross = row + (1 - 2 * z0) * NC * NQ * CHUNK
                    index = jnp.where(far[zp][c], blocks[cross : cross + 1, :], blocks[row : row + 1, :])
                    index = index.astype(jnp.int32)
                    index = jnp.broadcast_to(index, (8, LANES))
                    low = index & (LANES - 1)
                    level = [
                        jnp.take_along_axis(table[device * 8 + o], low, axis=1, mode="promise_in_bounds")
                        for o in range(OUTER)
                    ]
                    for place in range(3):
                        odd = (index & (ORDER << place)) != 0
                        level = [jnp.where(odd, level[k + 1], level[k]) for k in range(0, len(level), 2)]
                    same = ((index & LANES) != 0) == upper
                    picked.append(jnp.where(same, level[0], pltpu.roll(level[0], 4, 0)))
                rows.append(jnp.where(upper, picked[1], picked[0]))
            out[z0, 2 * zp, spot : spot + 8, :] = jnp.where(first, rows[0], rows[1])
            out[z0, 2 * zp + 1, spot : spot + 8, :] = jnp.where(first, rows[1], rows[0])


def zsum_kernel(scale, ids, blocks, out):
    zh = ids[0:1, :]
    odd = jnp.broadcast_to(zh, (8, LANES)) & 1 == 1
    signs = [jnp.broadcast_to(parity_sign(zh & d) * scale, (8, LANES)) for d in range(NZH)]
    for z0 in range(NZ0):
        for spot in range(0, NQ * COLS, 8):
            value = total([blocks[z0, d, spot : spot + 8, :] * signs[d] for d in range(NZH)])
            value = jnp.where(odd, pltpu.roll(value, SAMP, 1), value)
            out[z0 * NQ * COLS + spot : z0 * NQ * COLS + spot + 8, :] = value


def gram_kernel(ids, mine, other, sketch, gram):
    part = NQ * COLS
    zero = jnp.broadcast_to(ids[1:2, :], (part, LANES)) == 0
    pieces = []
    for z0 in range(NZ0):
        a, b = mine[z0 * part : (z0 + 1) * part, :], other[z0 * part : (z0 + 1) * part, :]
        pieces += [jnp.where(zero, a, b), jnp.where(zero, b, a)]
    low, high = jnp.concatenate(pieces[:2], axis=0), jnp.concatenate(pieces[2:], axis=0)
    value = jnp.concatenate([low, high], axis=0)
    zero = jnp.broadcast_to(ids[1:2, :], (W // NC, LANES)) == 0
    gram[...] = lax.dot_general(
        jnp.where(zero, low, high), value, (((1,), (1,)), ((), ())), precision=HIGHEST, preferred_element_type=F32
    )
    for tile, block in enumerate((low, high)):
        turned = block.T
        sketch[:, tile * LANES : (tile + 1) * LANES] = jnp.where(zero[:SAMP], turned[:SAMP], turned[SAMP:])


def spread_kernel(scale, blocks, out):
    value = total([blocks[k] for k in range(blocks.shape[0])]) * scale
    for k in range(out.shape[0]):
        out[k] = value


def factor_kernel(gram, rows_in, factor, rows_out, work):
    rows_out[...] = rows_in[...]
    work[...] = gram[...]
    sub = lax.broadcasted_iota(jnp.int32, (8, LANES), 0)
    lane = lax.broadcasted_iota(jnp.int32, (8, LANES), 1)
    block = 64
    for top in range(0, W, 8):
        at, tile = top % LANES, top // LANES
        spans = {t: slice(t * LANES, (t + 1) * LANES) for t in range(tile, W // LANES)}
        rows = [
            {t: jnp.broadcast_to(work[top + k : top + k + 1, span], (8, LANES)) for t, span in spans.items()}
            for k in range(8)
        ]
        head = [
            [None] * i + [jnp.broadcast_to(rows[i][tile][:, at + j : at + j + 1], (8, LANES)) for j in range(i, 8)]
            for i in range(8)
        ]
        inverse = []
        for k in range(8):
            inverse.append(lax.rsqrt(head[k][k]))
            for j in range(k + 1, 8):
                head[k][j] = head[k][j] * inverse[k]
            for t in spans:
                rows[k][t] = rows[k][t] * inverse[k]
            for i in range(k + 1, 8):
                for j in range(i, 8):
                    head[i][j] = head[i][j] - head[k][i] * head[k][j]
                for t in spans:
                    rows[i][t] = rows[i][t] - head[k][i] * rows[k][t]
        for t in range(tile):
            factor[top : top + 8, t * LANES : (t + 1) * LANES] = jnp.zeros((8, LANES), F32)
        for t, span in spans.items():
            value = rows[0][t]
            for k in range(1, 8):
                value = jnp.where(sub == k, rows[k][t], value)
            if t == tile:
                value = jnp.where(lane - at >= sub, value, 0.0)
            factor[top : top + 8, span] = value
        first = top // block * block
        last = first + block
        if top + 8 < last:
            for g in range(top + 8, last, 8):
                left = work[g : g + 8, spans[tile]]
                sides = [jnp.broadcast_to(left[:, at + j : at + j + 1], (8, LANES)) for j in range(8)]
                for k in range(8):
                    sides[k] = sides[k] * inverse[k]
                    for j in range(k + 1, 8):
                        sides[j] = sides[j] - sides[k] * head[k][j]
                for t, span in spans.items():
                    work[g : g + 8, span] = work[g : g + 8, span] - total([sides[k] * rows[k][t] for k in range(8)])
        elif last < W:
            start = last // LANES * LANES
            done = factor[first:last, start:]
            for a, b in ((last, last + block), (last + block, W)):
                if a < b:
                    work[a:b, start:] = work[a:b, start:] - lax.dot_general(
                        done[:, a - start : b - start],
                        done,
                        (((0,), (0,)), ((), ())),
                        precision=HIGHEST,
                        preferred_element_type=F32,
                    )


def on_device(matrix, signs, picks):
    zh, c = lax.axis_index("zh"), lax.axis_index("core")
    ids = jnp.broadcast_to(jnp.stack([zh, c]).astype(jnp.int32)[:, None], (2, LANES))
    matrix, ids = lax.optimization_barrier((matrix, ids))
    near = [lax.ppermute(picks, "zh", [(i, i ^ d) for i in range(NZH)]) for d in (1, 3)]
    far = lax.ppermute(picks, ("zh", "z0"), [(i, (i + 3 if i & 1 else i - 3) % NZ) for i in range(NZ)])
    line = [value.reshape(1, SAMP) for value in (picks, near[0], far, near[1])]

    table = pl.pallas_call(
        local_kernel,
        out_shape=shape(OUTER, W, ORDER),
        in_specs=[VMEM, VMEM],
        out_specs=VMEM,
        compiler_params=params(16),
        name="local",
    )(matrix, signs.reshape(OUTER * 2, LANES))
    packed = pl.pallas_call(
        pack_kernel,
        out_shape=shape(GROUP * CHUNK, LANES),
        in_specs=[VMEM] * 6,
        out_specs=VMEM,
        compiler_params=params(16),
        name="pack",
    )(ids, table, *[line[d] for d in LINE])
    packed = packed.reshape(GROUP, CHUNK // 2, 2, LANES)
    packed = lax.all_to_all(packed, ("z0", "core", "x", "y"), 0, 0, tiled=True).reshape(GROUP * CHUNK, LANES)

    sampled = pl.pallas_call(
        gather_kernel,
        out_shape=shape(NZ0, NZH, NQ * COLS, LANES),
        in_specs=[VMEM] * 2,
        out_specs=VMEM,
        scratch_shapes=[pltpu.VMEM((GROUP * OUTER, 8, LANES), F32)],
        compiler_params=params(16),
        name="gather",
    )(ids, packed)
    sampled = lax.all_to_all(
        sampled.reshape(CHIPS, COLS, LANES), ("z0", "zh", "x", "y"), 0, 0, tiled=True
    ).reshape(NZ0, NZH, NQ * COLS, LANES)

    mine = pl.pallas_call(
        lambda *refs: zsum_kernel(1.0 / math.sqrt(ROWS * 256), *refs),
        out_shape=shape(128, LANES),
        in_specs=[VMEM, VMEM],
        out_specs=VMEM,
        compiler_params=params(4),
        name="zsum",
    )(ids, sampled)
    other = lax.ppermute(mine, "core", [(0, 1), (1, 0)])
    sketch, gram = pl.pallas_call(
        gram_kernel,
        out_shape=[shape(SAMP, W), shape(W // NC, W)],
        in_specs=[VMEM, VMEM, VMEM],
        out_specs=[VMEM, VMEM],
        compiler_params=params(4),
        name="gram",
    )(ids, mine, other)

    def spread(blocks, count, scale, name):
        return pl.pallas_call(
            lambda *refs: spread_kernel(scale, *refs),
            out_shape=shape(count, 8, W),
            in_specs=[VMEM],
            out_specs=VMEM,
            compiler_params=params(4),
            name=name,
        )(blocks)

    gram = lax.all_to_all(gram.reshape(NQ, 8, W), ("x", "y"), 0, 0, tiled=True)
    rows = spread(gram, NZ, 1.0, "sum_xy")
    rows = lax.all_to_all(rows, ("z0", "zh"), 0, 0, tiled=True)
    rows = spread(rows, NC * NQ, 1.0 / (SAMP * 256), "sum_z")
    gram = lax.all_to_all(rows, ("core", "x", "y"), 0, 0, tiled=True).reshape(W, W)
    factor, sketch = pl.pallas_call(
        factor_kernel,
        out_shape=[shape(W, W), shape(SAMP, W)],
        in_specs=[VMEM, VMEM],
        out_specs=[VMEM, VMEM],
        scratch_shapes=[pltpu.VMEM((W, W), F32)],
        compiler_params=params(4),
        name="factor",
    )(gram, sketch)
    return (sketch, factor)


def solution(mesh):
    devices = mesh.devices.transpose([mesh.axis_names.index(name) for name in ("rows", "grp")])
    split = Mesh(devices.reshape(NX, NZH, NZ0, NC, NY), ("x", "zh", "z0", "core", "y"))
    rows = ("y", "x", "zh", "z0", "core")
    return jax.shard_map(
        on_device,
        mesh=split,
        in_specs=(P(rows, None), P(rows), P(rows)),
        out_specs=(P(rows, None), P()),
        check_vma=False,
    )
```

```python
import math

import jax
import jax.numpy as jnp
from jax import lax
from jax.experimental import pallas as pl
from jax.experimental.pallas import tpu as pltpu
from jax.sharding import Mesh, PartitionSpec as P

NX, NZH, NZ0, NC, NY = 4, 4, 2, 2, 4
NZ = NZH * NZ0
NQ = NX * NY
ROWS = 2048
SAMP = 64
OUTER = 8
ORDER = 256
W = 256
GROUP = NC * NZ0 * NX * NY
COLS = W // GROUP
CHUNK = OUTER * 8 + 2
CHIPS = NZH * NZ0 * NX * NY
LANES = 128
LINE = (0, 2, 1, 3)
F32 = jnp.float32
HIGHEST = lax.Precision.HIGHEST
VMEM = pl.BlockSpec(memory_space=pltpu.VMEM)


def params(mib):
    return pltpu.CompilerParams(vmem_limit_bytes=mib * 1024 * 1024)


def shape(*sizes):
    return jax.ShapeDtypeStruct(sizes, F32)


def parity_sign(value):
    return (1 - 2 * ((value ^ (value >> 1)) & 1)).astype(F32)


def butterfly(values):
    values = list(values)
    half = 1
    while half < len(values):
        for first in range(len(values)):
            if first & half == 0:
                a, b = values[first], values[first | half]
                values[first], values[first | half] = a + b, a - b
        half *= 2
    return values


def total(parts):
    while len(parts) > 1:
        parts = [parts[k] + parts[k + 1] for k in range(0, len(parts), 2)]
    return parts[0]


def local_kernel(matrix, signs, table):
    row = lax.broadcasted_iota(jnp.int32, (ORDER, ORDER), 0)
    col = lax.broadcasted_iota(jnp.int32, (ORDER, ORDER), 1)
    both = row & col
    both = both ^ (both >> 4)
    both = both ^ (both >> 2)
    both = both ^ (both >> 1)
    hadamard = (1 - 2 * (both & 1)).astype(F32).astype(jnp.bfloat16)
    for o in range(OUTER):
        block = matrix[o * ORDER : (o + 1) * ORDER, :].astype(F32)
        sign = jnp.concatenate([signs[2 * o : 2 * o + 1, :], signs[2 * o + 1 : 2 * o + 2, :]], axis=1)
        flipped = (block.T * sign.astype(F32)).astype(jnp.bfloat16)
        table[o] = jnp.dot(flipped, hadamard, preferred_element_type=F32)


def pack_kernel(ids, table, p0, p1, p2, p3, out):
    sub = lax.broadcasted_iota(jnp.int32, (8, LANES), 0)
    for o in range(OUTER):
        for pair in range(GROUP // 2):
            low = table[o, pair * 8 : pair * 8 + 8, :LANES]
            high = table[o, pair * 8 : pair * 8 + 8, LANES:]
            spot = 2 * pair * CHUNK + o * 8
            out[spot : spot + 8, :] = jnp.where(sub < 4, low, pltpu.roll(high, 4, 0))
            spot += CHUNK
            out[spot : spot + 8, :] = jnp.where(sub < 4, pltpu.roll(low, 4, 0), high)
    zh, c = ids[0:1, :], ids[1:2, :]
    row = lax.broadcasted_iota(jnp.int32, (2, LANES), 0)
    lane = lax.broadcasted_iota(jnp.int32, (2, LANES), 1)
    tile = jnp.zeros((2, LANES), F32)
    for d, ref in zip(LINE, (p0, p1, p2, p3)):
        place = zh ^ d
        value = (ref[...] & (ROWS - 1)).astype(F32)
        value = jnp.broadcast_to(jnp.concatenate([value, value], axis=1), (2, LANES))
        here = (row == (place >> 1)) & ((lane >> 6) == ((place & 1) ^ c))
        tile = jnp.where(here, value, tile)
    for k in range(GROUP):
        out[k * CHUNK + OUTER * 8 : (k + 1) * CHUNK, :] = tile


def gather_kernel(ids, blocks, out, table):
    for high in range(32):
        values = [blocks[(high * 2 + low) * CHUNK + o * 8 : (high * 2 + low) * CHUNK + o * 8 + 8, :] for low in range(2) for o in range(OUTER)]
        for k, value in enumerate(butterfly(values)):
            table[high * 16 + k] = value
    for rest in range(16):
        values = [table[high * 16 + rest] for high in range(32)]
        for high, value in enumerate(butterfly(values)):
            table[high * 16 + rest] = value
    sub = lax.broadcasted_iota(jnp.int32, (8, LANES), 0)
    lane = lax.broadcasted_iota(jnp.int32, (8, LANES), 1)
    upper, first = sub >= 4, lane < SAMP
    zh, half_lane = ids[0:1, :], lane[0:1, :] >> 6
    far = [[((zh >> 1) != zp) & (half_lane == ((zh & 1) ^ c)) for c in range(NC)] for zp in range(2)]
    for half in range(GROUP // 4):
        z0, spot = half // (NQ // 2), half % (NQ // 2) * 8
        for zp in range(2):
            rows = []
            for c in range(NC):
                picked = []
                for ylo in range(2):
                    device = (z0 * NC + c) * NQ + spot // 4 + ylo
                    row = device * CHUNK + OUTER * 8 + zp
                    cross = row + (1 - 2 * z0) * NC * NQ * CHUNK
                    index = jnp.where(far[zp][c], blocks[cross : cross + 1, :], blocks[row : row + 1, :])
                    index = index.astype(jnp.int32)
                    index = jnp.broadcast_to(index, (8, LANES))
                    low = index & (LANES - 1)
                    level = [
                        jnp.take_along_axis(table[device * 8 + o], low, axis=1, mode="promise_in_bounds")
                        for o in range(OUTER)
                    ]
                    for place in range(3):
                        odd = (index & (ORDER << place)) != 0
                        level = [jnp.where(odd, level[k + 1], level[k]) for k in range(0, len(level), 2)]
                    same = ((index & LANES) != 0) == upper
                    picked.append(jnp.where(same, level[0], pltpu.roll(level[0], 4, 0)))
                rows.append(jnp.where(upper, picked[1], picked[0]))
            out[z0, 2 * zp, spot : spot + 8, :] = jnp.where(first, rows[0], rows[1])
            out[z0, 2 * zp + 1, spot : spot + 8, :] = jnp.where(first, rows[1], rows[0])


def zsum_kernel(scale, ids, blocks, out):
    zh = ids[0:1, :]
    odd = jnp.broadcast_to(zh, (8, LANES)) & 1 == 1
    signs = [jnp.broadcast_to(parity_sign(zh & d) * scale, (8, LANES)) for d in range(NZH)]
    for z0 in range(NZ0):
        for spot in range(0, NQ * COLS, 8):
            value = total([blocks[z0, d, spot : spot + 8, :] * signs[d] for d in range(NZH)])
            value = jnp.where(odd, pltpu.roll(value, SAMP, 1), value)
            out[z0 * NQ * COLS + spot : z0 * NQ * COLS + spot + 8, :] = value


def gram_kernel(ids, mine, other, sketch, gram):
    part = NQ * COLS
    zero = jnp.broadcast_to(ids[1:2, :], (part, LANES)) == 0
    pieces = []
    for z0 in range(NZ0):
        a, b = mine[z0 * part : (z0 + 1) * part, :], other[z0 * part : (z0 + 1) * part, :]
        pieces += [jnp.where(zero, a, b), jnp.where(zero, b, a)]
    low, high = jnp.concatenate(pieces[:2], axis=0), jnp.concatenate(pieces[2:], axis=0)
    value = jnp.concatenate([low, high], axis=0)
    zero = jnp.broadcast_to(ids[1:2, :], (W // NC, LANES)) == 0
    gram[...] = lax.dot_general(
        jnp.where(zero, low, high), value, (((1,), (1,)), ((), ())), precision=HIGHEST, preferred_element_type=F32
    )
    for tile, block in enumerate((low, high)):
        turned = block.T
        sketch[:, tile * LANES : (tile + 1) * LANES] = jnp.where(zero[:SAMP], turned[:SAMP], turned[SAMP:])


def spread_kernel(scale, blocks, out):
    value = total([blocks[k] for k in range(blocks.shape[0])]) * scale
    for k in range(out.shape[0]):
        out[k] = value


def factor_kernel(ids, mine, other, rows_in, factor, rows_out, work):
    rows_out[...] = rows_in[...]
    zero = jnp.broadcast_to(ids[1:2, :], (W // NC, LANES)) == 0
    for t in range(W // LANES):
        span = slice(t * LANES, (t + 1) * LANES)
        work[: W // NC, span] = jnp.where(zero, mine[:, span], other[:, span])
        work[W // NC :, span] = jnp.where(zero, other[:, span], mine[:, span])
    sub = lax.broadcasted_iota(jnp.int32, (8, LANES), 0)
    lane = lax.broadcasted_iota(jnp.int32, (8, LANES), 1)
    block = 64
    for top in range(0, W, 8):
        at, tile = top % LANES, top // LANES
        spans = {t: slice(t * LANES, (t + 1) * LANES) for t in range(tile, W // LANES)}
        rows = [
            {t: jnp.broadcast_to(work[top + k : top + k + 1, span], (8, LANES)) for t, span in spans.items()}
            for k in range(8)
        ]
        head = [
            [None] * i + [jnp.broadcast_to(rows[i][tile][:, at + j : at + j + 1], (8, LANES)) for j in range(i, 8)]
            for i in range(8)
        ]
        inverse = []
        for k in range(8):
            inverse.append(lax.rsqrt(head[k][k]))
            for j in range(k + 1, 8):
                head[k][j] = head[k][j] * inverse[k]
            for t in spans:
                rows[k][t] = rows[k][t] * inverse[k]
            for i in range(k + 1, 8):
                for j in range(i, 8):
                    head[i][j] = head[i][j] - head[k][i] * head[k][j]
                for t in spans:
                    rows[i][t] = rows[i][t] - head[k][i] * rows[k][t]
        for t in range(tile):
            factor[top : top + 8, t * LANES : (t + 1) * LANES] = jnp.zeros((8, LANES), F32)
        for t, span in spans.items():
            value = rows[0][t]
            for k in range(1, 8):
                value = jnp.where(sub == k, rows[k][t], value)
            if t == tile:
                value = jnp.where(lane - at >= sub, value, 0.0)
            factor[top : top + 8, span] = value
        first = top // block * block
        last = first + block
        if top + 8 < last:
            for g in range(top + 8, last, 8):
                left = work[g : g + 8, spans[tile]]
                sides = [jnp.broadcast_to(left[:, at + j : at + j + 1], (8, LANES)) for j in range(8)]
                for k in range(8):
                    sides[k] = sides[k] * inverse[k]
                    for j in range(k + 1, 8):
                        sides[j] = sides[j] - sides[k] * head[k][j]
                for t, span in spans.items():
                    work[g : g + 8, span] = work[g : g + 8, span] - total([sides[k] * rows[k][t] for k in range(8)])
        elif last < W:
            start = last // LANES * LANES
            done = factor[first:last, start:]
            for a, b in ((last, last + block), (last + block, W)):
                if a < b:
                    work[a:b, start:] = work[a:b, start:] - lax.dot_general(
                        done[:, a - start : b - start],
                        done,
                        (((0,), (0,)), ((), ())),
                        precision=HIGHEST,
                        preferred_element_type=F32,
                    )


def on_device(matrix, signs, picks):
    zh, c = lax.axis_index("zh"), lax.axis_index("core")
    ids = jnp.broadcast_to(jnp.stack([zh, c]).astype(jnp.int32)[:, None], (2, LANES))
    matrix, ids = lax.optimization_barrier((matrix, ids))
    near = [lax.ppermute(picks, "zh", [(i, i ^ d) for i in range(NZH)]) for d in (1, 3)]
    far = lax.ppermute(picks, ("zh", "z0"), [(i, (i + 3 if i & 1 else i - 3) % NZ) for i in range(NZ)])
    line = [value.reshape(1, SAMP) for value in (picks, near[0], far, near[1])]

    table = pl.pallas_call(
        local_kernel,
        out_shape=shape(OUTER, W, ORDER),
        in_specs=[VMEM, VMEM],
        out_specs=VMEM,
        compiler_params=params(16),
        name="local",
    )(matrix, signs.reshape(OUTER * 2, LANES))
    packed = pl.pallas_call(
        pack_kernel,
        out_shape=shape(GROUP * CHUNK, LANES),
        in_specs=[VMEM] * 6,
        out_specs=VMEM,
        compiler_params=params(16),
        name="pack",
    )(ids, table, *[line[d] for d in LINE])
    packed = packed.reshape(GROUP, CHUNK // 2, 2, LANES)
    packed = lax.all_to_all(packed, ("z0", "core", "x", "y"), 0, 0, tiled=True).reshape(GROUP * CHUNK, LANES)

    sampled = pl.pallas_call(
        gather_kernel,
        out_shape=shape(NZ0, NZH, NQ * COLS, LANES),
        in_specs=[VMEM] * 2,
        out_specs=VMEM,
        scratch_shapes=[pltpu.VMEM((GROUP * OUTER, 8, LANES), F32)],
        compiler_params=params(16),
        name="gather",
    )(ids, packed)
    sampled = lax.all_to_all(
        sampled.reshape(CHIPS, COLS, LANES), ("z0", "zh", "x", "y"), 0, 0, tiled=True
    ).reshape(NZ0, NZH, NQ * COLS, LANES)

    mine = pl.pallas_call(
        lambda *refs: zsum_kernel(1.0 / math.sqrt(ROWS * 256), *refs),
        out_shape=shape(128, LANES),
        in_specs=[VMEM, VMEM],
        out_specs=VMEM,
        compiler_params=params(4),
        name="zsum",
    )(ids, sampled)
    other = lax.ppermute(mine, "core", [(0, 1), (1, 0)])
    sketch, gram = pl.pallas_call(
        gram_kernel,
        out_shape=[shape(SAMP, W), shape(W // NC, W)],
        in_specs=[VMEM, VMEM, VMEM],
        out_specs=[VMEM, VMEM],
        compiler_params=params(4),
        name="gram",
    )(ids, mine, other)

    def spread(blocks, count, scale, name):
        return pl.pallas_call(
            lambda *refs: spread_kernel(scale, *refs),
            out_shape=shape(count, 8, W),
            in_specs=[VMEM],
            out_specs=VMEM,
            compiler_params=params(4),
            name=name,
        )(blocks)

    gram = lax.all_to_all(gram.reshape(NQ, 8, W), ("x", "y"), 0, 0, tiled=True)
    rows = spread(gram, NZ, 1.0, "sum_xy")
    rows = lax.all_to_all(rows, ("z0", "zh"), 0, 0, tiled=True)
    rows = spread(rows, NQ, 1.0 / (SAMP * 256), "sum_z")
    mine = lax.all_to_all(rows, ("x", "y"), 0, 0, tiled=True).reshape(W // NC, W)
    other = lax.ppermute(mine, "core", [(0, 1), (1, 0)])
    factor, sketch = pl.pallas_call(
        factor_kernel,
        out_shape=[shape(W, W), shape(SAMP, W)],
        in_specs=[VMEM] * 4,
        out_specs=[VMEM, VMEM],
        scratch_shapes=[pltpu.VMEM((W, W), F32)],
        compiler_params=params(4),
        name="factor",
    )(ids, mine, other, sketch)
    return (sketch, factor)


def solution(mesh):
    devices = mesh.devices.transpose([mesh.axis_names.index(name) for name in ("rows", "grp")])
    split = Mesh(devices.reshape(NX, NZH, NZ0, NC, NY), ("x", "zh", "z0", "core", "y"))
    rows = ("y", "x", "zh", "z0", "core")
    return jax.shard_map(
        on_device,
        mesh=split,
        in_specs=(P(rows, None), P(rows), P(rows)),
        out_specs=(P(rows, None), P()),
        check_vma=False,
    )
```

```python
import math

import jax
import jax.numpy as jnp
from jax import lax
from jax.experimental import pallas as pl
from jax.experimental.pallas import tpu as pltpu
from jax.sharding import Mesh, PartitionSpec as P

NX, NZH, NZ0, NC, NY = 4, 4, 2, 2, 4
NZ = NZH * NZ0
NQ = NX * NY
ROWS = 2048
SAMP = 64
OUTER = 8
ORDER = 256
W = 256
GROUP = NC * NZ0 * NX * NY
COLS = W // GROUP
CHUNK = OUTER * 8 + 2
CHIPS = NZH * NZ0 * NX * NY
LANES = 128
LINE = (0, 2, 1, 3)
F32 = jnp.float32
HIGHEST = lax.Precision.HIGHEST
HBM = pl.BlockSpec(memory_space=pltpu.HBM)
VMEM = pl.BlockSpec(memory_space=pltpu.VMEM)


def params(mib):
    return pltpu.CompilerParams(vmem_limit_bytes=mib * 1024 * 1024)


def pinned(value):
    return pltpu.with_memory_space_constraint(value, pltpu.HBM)


def shape(*sizes):
    return jax.ShapeDtypeStruct(sizes, F32)


def parity_sign(value):
    return (1 - 2 * ((value ^ (value >> 1)) & 1)).astype(F32)


def butterfly(values):
    values = list(values)
    half = 1
    while half < len(values):
        for first in range(len(values)):
            if first & half == 0:
                a, b = values[first], values[first | half]
                values[first], values[first | half] = a + b, a - b
        half *= 2
    return values


def total(parts):
    while len(parts) > 1:
        parts = [parts[k] + parts[k + 1] for k in range(0, len(parts), 2)]
    return parts[0]


def local_kernel(matrix, signs, table, rows, marks, row_sems, mark_sem):
    half = OUTER // 2
    blocks = [pl.ds(o * ORDER, half * ORDER) for o in range(0, OUTER, half)]
    fetches = [pltpu.make_async_copy(matrix.at[b], rows.at[b], row_sems.at[o]) for o, b in enumerate(blocks)]
    mark = pltpu.make_async_copy(signs, marks, mark_sem)
    mark.start()
    for fetch in fetches:
        fetch.start()
    row = lax.broadcasted_iota(jnp.int32, (ORDER, ORDER), 0)
    col = lax.broadcasted_iota(jnp.int32, (ORDER, ORDER), 1)
    both = row & col
    both = both ^ (both >> 4)
    both = both ^ (both >> 2)
    both = both ^ (both >> 1)
    hadamard = (1 - 2 * (both & 1)).astype(F32).astype(jnp.bfloat16)
    mark.wait()
    for o in range(OUTER):
        if o % half == 0:
            fetches[o // half].wait()
        block = rows[o * ORDER : (o + 1) * ORDER, :].astype(F32)
        sign = jnp.concatenate([marks[2 * o : 2 * o + 1, :], marks[2 * o + 1 : 2 * o + 2, :]], axis=1)
        flipped = (block.T * sign.astype(F32)).astype(jnp.bfloat16)
        table[o] = jnp.dot(flipped, hadamard, preferred_element_type=F32)


def pack_kernel(ids, table, p0, p1, p2, p3, out):
    sub = lax.broadcasted_iota(jnp.int32, (8, LANES), 0)
    for o in range(OUTER):
        for pair in range(GROUP // 2):
            low = table[o, pair * 8 : pair * 8 + 8, :LANES]
            high = table[o, pair * 8 : pair * 8 + 8, LANES:]
            spot = 2 * pair * CHUNK + o * 8
            out[spot : spot + 8, :] = jnp.where(sub < 4, low, pltpu.roll(high, 4, 0))
            spot += CHUNK
            out[spot : spot + 8, :] = jnp.where(sub < 4, pltpu.roll(low, 4, 0), high)
    zh, c = ids[0:1, :], ids[1:2, :]
    row = lax.broadcasted_iota(jnp.int32, (2, LANES), 0)
    lane = lax.broadcasted_iota(jnp.int32, (2, LANES), 1)
    tile = jnp.zeros((2, LANES), F32)
    for d, ref in zip(LINE, (p0, p1, p2, p3)):
        place = zh ^ d
        value = (ref[...] & (ROWS - 1)).astype(F32)
        value = jnp.broadcast_to(jnp.concatenate([value, value], axis=1), (2, LANES))
        here = (row == (place >> 1)) & ((lane >> 6) == ((place & 1) ^ c))
        tile = jnp.where(here, value, tile)
    for k in range(GROUP):
        out[k * CHUNK + OUTER * 8 : (k + 1) * CHUNK, :] = tile


def gather_kernel(ids, blocks, out, table):
    for high in range(32):
        values = [blocks[(high * 2 + low) * CHUNK + o * 8 : (high * 2 + low) * CHUNK + o * 8 + 8, :] for low in range(2) for o in range(OUTER)]
        for k, value in enumerate(butterfly(values)):
            table[high * 16 + k] = value
    for rest in range(16):
        values = [table[high * 16 + rest] for high in range(32)]
        for high, value in enumerate(butterfly(values)):
            table[high * 16 + rest] = value
    sub = lax.broadcasted_iota(jnp.int32, (8, LANES), 0)
    lane = lax.broadcasted_iota(jnp.int32, (8, LANES), 1)
    upper, first = sub >= 4, lane < SAMP
    zh, half_lane = ids[0:1, :], lane[0:1, :] >> 6
    far = [[((zh >> 1) != zp) & (half_lane == ((zh & 1) ^ c)) for c in range(NC)] for zp in range(2)]
    for half in range(GROUP // 4):
        z0, spot = half // (NQ // 2), half % (NQ // 2) * 8
        for zp in range(2):
            rows = []
            for c in range(NC):
                picked = []
                for ylo in range(2):
                    device = (z0 * NC + c) * NQ + spot // 4 + ylo
                    row = device * CHUNK + OUTER * 8 + zp
                    cross = row + (1 - 2 * z0) * NC * NQ * CHUNK
                    index = jnp.where(far[zp][c], blocks[cross : cross + 1, :], blocks[row : row + 1, :])
                    index = index.astype(jnp.int32)
                    index = jnp.broadcast_to(index, (8, LANES))
                    low = index & (LANES - 1)
                    level = [
                        jnp.take_along_axis(table[device * 8 + o], low, axis=1, mode="promise_in_bounds")
                        for o in range(OUTER)
                    ]
                    for place in range(3):
                        odd = (index & (ORDER << place)) != 0
                        level = [jnp.where(odd, level[k + 1], level[k]) for k in range(0, len(level), 2)]
                    same = ((index & LANES) != 0) == upper
                    picked.append(jnp.where(same, level[0], pltpu.roll(level[0], 4, 0)))
                rows.append(jnp.where(upper, picked[1], picked[0]))
            out[z0, 2 * zp, spot : spot + 8, :] = jnp.where(first, rows[0], rows[1])
            out[z0, 2 * zp + 1, spot : spot + 8, :] = jnp.where(first, rows[1], rows[0])


def zsum_kernel(scale, ids, blocks, out):
    zh = ids[0:1, :]
    odd = jnp.broadcast_to(zh, (8, LANES)) & 1 == 1
    signs = [jnp.broadcast_to(parity_sign(zh & d) * scale, (8, LANES)) for d in range(NZH)]
    for z0 in range(NZ0):
        for spot in range(0, NQ * COLS, 8):
            value = total([blocks[z0, d, spot : spot + 8, :] * signs[d] for d in range(NZH)])
            value = jnp.where(odd, pltpu.roll(value, SAMP, 1), value)
            out[z0 * NQ * COLS + spot : z0 * NQ * COLS + spot + 8, :] = value


def gram_kernel(ids, mine, other, sketch, gram):
    part = NQ * COLS
    zero = jnp.broadcast_to(ids[1:2, :], (part, LANES)) == 0
    pieces = []
    for z0 in range(NZ0):
        a, b = mine[z0 * part : (z0 + 1) * part, :], other[z0 * part : (z0 + 1) * part, :]
        pieces += [jnp.where(zero, a, b), jnp.where(zero, b, a)]
    low, high = jnp.concatenate(pieces[:2], axis=0), jnp.concatenate(pieces[2:], axis=0)
    value = jnp.concatenate([low, high], axis=0)
    zero = jnp.broadcast_to(ids[1:2, :], (W // NC, LANES)) == 0
    gram[...] = lax.dot_general(
        jnp.where(zero, low, high), value, (((1,), (1,)), ((), ())), precision=HIGHEST, preferred_element_type=F32
    )
    for tile, block in enumerate((low, high)):
        turned = block.T
        sketch[:, tile * LANES : (tile + 1) * LANES] = jnp.where(zero[:SAMP], turned[:SAMP], turned[SAMP:])


def spread_kernel(scale, blocks, out):
    value = total([blocks[k] for k in range(blocks.shape[0])]) * scale
    for k in range(out.shape[0]):
        out[k] = value


def factor_kernel(ids, mine, other, rows_in, factor, rows_out, work):
    rows_out[...] = rows_in[...]
    zero = jnp.broadcast_to(ids[1:2, :], (W // NC, LANES)) == 0
    for t in range(W // LANES):
        span = slice(t * LANES, (t + 1) * LANES)
        work[: W // NC, span] = jnp.where(zero, mine[:, span], other[:, span])
        work[W // NC :, span] = jnp.where(zero, other[:, span], mine[:, span])
    sub = lax.broadcasted_iota(jnp.int32, (8, LANES), 0)
    lane = lax.broadcasted_iota(jnp.int32, (8, LANES), 1)
    block = 64
    for top in range(0, W, 8):
        at, tile = top % LANES, top // LANES
        spans = {t: slice(t * LANES, (t + 1) * LANES) for t in range(tile, W // LANES)}
        rows = [
            {t: jnp.broadcast_to(work[top + k : top + k + 1, span], (8, LANES)) for t, span in spans.items()}
            for k in range(8)
        ]
        head = [
            [None] * i + [jnp.broadcast_to(rows[i][tile][:, at + j : at + j + 1], (8, LANES)) for j in range(i, 8)]
            for i in range(8)
        ]
        inverse = []
        for k in range(8):
            inverse.append(lax.rsqrt(head[k][k]))
            for j in range(k + 1, 8):
                head[k][j] = head[k][j] * inverse[k]
            for t in spans:
                rows[k][t] = rows[k][t] * inverse[k]
            for i in range(k + 1, 8):
                for j in range(i, 8):
                    head[i][j] = head[i][j] - head[k][i] * head[k][j]
                for t in spans:
                    rows[i][t] = rows[i][t] - head[k][i] * rows[k][t]
        for t in range(tile):
            factor[top : top + 8, t * LANES : (t + 1) * LANES] = jnp.zeros((8, LANES), F32)
        for t, span in spans.items():
            value = rows[0][t]
            for k in range(1, 8):
                value = jnp.where(sub == k, rows[k][t], value)
            if t == tile:
                value = jnp.where(lane - at >= sub, value, 0.0)
            factor[top : top + 8, span] = value
        first = top // block * block
        last = first + block
        if top + 8 < last:
            for g in range(top + 8, last, 8):
                left = work[g : g + 8, spans[tile]]
                sides = [jnp.broadcast_to(left[:, at + j : at + j + 1], (8, LANES)) for j in range(8)]
                for k in range(8):
                    sides[k] = sides[k] * inverse[k]
                    for j in range(k + 1, 8):
                        sides[j] = sides[j] - sides[k] * head[k][j]
                for t, span in spans.items():
                    work[g : g + 8, span] = work[g : g + 8, span] - total([sides[k] * rows[k][t] for k in range(8)])
        elif last < W:
            start = last // LANES * LANES
            done = factor[first:last, start:]
            for a, b in ((last, last + block), (last + block, W)):
                if a < b:
                    work[a:b, start:] = work[a:b, start:] - lax.dot_general(
                        done[:, a - start : b - start],
                        done,
                        (((0,), (0,)), ((), ())),
                        precision=HIGHEST,
                        preferred_element_type=F32,
                    )


def on_device(matrix, signs, picks):
    zh, c = lax.axis_index("zh"), lax.axis_index("core")
    ids = jnp.broadcast_to(jnp.stack([zh, c]).astype(jnp.int32)[:, None], (2, LANES))
    matrix, ids = lax.optimization_barrier((matrix, ids))
    near = [lax.ppermute(picks, "zh", [(i, i ^ d) for i in range(NZH)]) for d in (1, 3)]
    far = lax.ppermute(picks, ("zh", "z0"), [(i, (i + 3 if i & 1 else i - 3) % NZ) for i in range(NZ)])
    line = [value.reshape(1, SAMP) for value in (picks, near[0], far, near[1])]

    table = pl.pallas_call(
        local_kernel,
        out_shape=shape(OUTER, W, ORDER),
        in_specs=[HBM, HBM],
        out_specs=VMEM,
        scratch_shapes=[
            pltpu.VMEM((ROWS, W), jnp.bfloat16),
            pltpu.VMEM((OUTER * 2, LANES), jnp.int32),
            pltpu.SemaphoreType.DMA((2,)),
            pltpu.SemaphoreType.DMA,
        ],
        compiler_params=params(16),
        name="local",
    )(pinned(matrix), pinned(signs.reshape(OUTER * 2, LANES)))
    packed = pl.pallas_call(
        pack_kernel,
        out_shape=shape(GROUP * CHUNK, LANES),
        in_specs=[VMEM] * 6,
        out_specs=VMEM,
        compiler_params=params(16),
        name="pack",
    )(ids, table, *[line[d] for d in LINE])
    packed = packed.reshape(GROUP, CHUNK // 2, 2, LANES)
    packed = lax.all_to_all(packed, ("z0", "core", "x", "y"), 0, 0, tiled=True).reshape(GROUP * CHUNK, LANES)

    sampled = pl.pallas_call(
        gather_kernel,
        out_shape=shape(NZ0, NZH, NQ * COLS, LANES),
        in_specs=[VMEM] * 2,
        out_specs=VMEM,
        scratch_shapes=[pltpu.VMEM((GROUP * OUTER, 8, LANES), F32)],
        compiler_params=params(16),
        name="gather",
    )(ids, packed)
    sampled = lax.all_to_all(
        sampled.reshape(CHIPS, COLS, LANES), ("z0", "zh", "x", "y"), 0, 0, tiled=True
    ).reshape(NZ0, NZH, NQ * COLS, LANES)

    mine = pl.pallas_call(
        lambda *refs: zsum_kernel(1.0 / math.sqrt(ROWS * 256), *refs),
        out_shape=shape(128, LANES),
        in_specs=[VMEM, VMEM],
        out_specs=VMEM,
        compiler_params=params(4),
        name="zsum",
    )(ids, sampled)
    other = lax.ppermute(mine, "core", [(0, 1), (1, 0)])
    sketch, gram = pl.pallas_call(
        gram_kernel,
        out_shape=[shape(SAMP, W), shape(W // NC, W)],
        in_specs=[VMEM, VMEM, VMEM],
        out_specs=[VMEM, VMEM],
        compiler_params=params(4),
        name="gram",
    )(ids, mine, other)

    def spread(blocks, count, scale, name):
        return pl.pallas_call(
            lambda *refs: spread_kernel(scale, *refs),
            out_shape=shape(count, 8, W),
            in_specs=[VMEM],
            out_specs=VMEM,
            compiler_params=params(4),
            name=name,
        )(blocks)

    gram = lax.all_to_all(gram.reshape(NQ, 8, W), ("x", "y"), 0, 0, tiled=True)
    rows = spread(gram, NZ, 1.0, "sum_xy")
    rows = lax.all_to_all(rows, ("z0", "zh"), 0, 0, tiled=True)
    rows = spread(rows, NQ, 1.0 / (SAMP * 256), "sum_z")
    mine = lax.all_to_all(rows, ("x", "y"), 0, 0, tiled=True).reshape(W // NC, W)
    other = lax.ppermute(mine, "core", [(0, 1), (1, 0)])
    factor, sketch = pl.pallas_call(
        factor_kernel,
        out_shape=[shape(W, W), shape(SAMP, W)],
        in_specs=[VMEM] * 4,
        out_specs=[VMEM, VMEM],
        scratch_shapes=[pltpu.VMEM((W, W), F32)],
        compiler_params=params(4),
        name="factor",
    )(ids, mine, other, sketch)
    return (sketch, factor)


def solution(mesh):
    devices = mesh.devices.transpose([mesh.axis_names.index(name) for name in ("rows", "grp")])
    split = Mesh(devices.reshape(NX, NZH, NZ0, NC, NY), ("x", "zh", "z0", "core", "y"))
    rows = ("y", "x", "zh", "z0", "core")
    return jax.shard_map(
        on_device,
        mesh=split,
        in_specs=(P(rows, None), P(rows), P(rows)),
        out_specs=(P(rows, None), P()),
        check_vma=False,
    )
```

```python
import math

import jax
import jax.numpy as jnp
from jax import lax
from jax.experimental import pallas as pl
from jax.experimental.pallas import tpu as pltpu
from jax.sharding import Mesh, PartitionSpec as P

NX, NZH, NZ0, NC, NY = 4, 4, 2, 2, 4
NZ = NZH * NZ0
NQ = NX * NY
ROWS = 2048
SAMP = 64
OUTER = 8
ORDER = 256
W = 256
GROUP = NC * NZ0 * NX * NY
COLS = W // GROUP
CHUNK = OUTER * 8 + 2
CHIPS = NZH * NZ0 * NX * NY
LANES = 128
LINE = (0, 2, 3, 1)
F32 = jnp.float32
HIGHEST = lax.Precision.HIGHEST
HBM = pl.BlockSpec(memory_space=pltpu.HBM)
VMEM = pl.BlockSpec(memory_space=pltpu.VMEM)


def params(mib):
    return pltpu.CompilerParams(vmem_limit_bytes=mib * 1024 * 1024)


def pinned(value):
    return pltpu.with_memory_space_constraint(value, pltpu.HBM)


def shape(*sizes):
    return jax.ShapeDtypeStruct(sizes, F32)


def parity_sign(value):
    return (1 - 2 * ((value ^ (value >> 1)) & 1)).astype(F32)


def butterfly(values):
    values = list(values)
    half = 1
    while half < len(values):
        for first in range(len(values)):
            if first & half == 0:
                a, b = values[first], values[first | half]
                values[first], values[first | half] = a + b, a - b
        half *= 2
    return values


def total(parts):
    while len(parts) > 1:
        parts = [parts[k] + parts[k + 1] for k in range(0, len(parts), 2)]
    return parts[0]


def local_kernel(matrix, signs, table, rows, marks, row_sems, mark_sem):
    half = OUTER // 2
    blocks = [pl.ds(o * ORDER, half * ORDER) for o in range(0, OUTER, half)]
    fetches = [pltpu.make_async_copy(matrix.at[b], rows.at[b], row_sems.at[o]) for o, b in enumerate(blocks)]
    mark = pltpu.make_async_copy(signs, marks, mark_sem)
    mark.start()
    for fetch in fetches:
        fetch.start()
    row = lax.broadcasted_iota(jnp.int32, (ORDER, ORDER), 0)
    col = lax.broadcasted_iota(jnp.int32, (ORDER, ORDER), 1)
    both = row & col
    both = both ^ (both >> 4)
    both = both ^ (both >> 2)
    both = both ^ (both >> 1)
    hadamard = (1 - 2 * (both & 1)).astype(F32).astype(jnp.bfloat16)
    mark.wait()
    for o in range(OUTER):
        if o % half == 0:
            fetches[o // half].wait()
        block = rows[o * ORDER : (o + 1) * ORDER, :].astype(F32)
        sign = jnp.concatenate([marks[2 * o : 2 * o + 1, :], marks[2 * o + 1 : 2 * o + 2, :]], axis=1)
        flipped = (block.T * sign.astype(F32)).astype(jnp.bfloat16)
        table[o] = jnp.dot(flipped, hadamard, preferred_element_type=F32)


def pack_kernel(ids, table, p0, p1, p2, p3, out):
    sub = lax.broadcasted_iota(jnp.int32, (8, LANES), 0)
    for o in range(OUTER):
        for pair in range(GROUP // 2):
            low = table[o, pair * 8 : pair * 8 + 8, :LANES]
            high = table[o, pair * 8 : pair * 8 + 8, LANES:]
            spot = 2 * pair * CHUNK + o * 8
            out[spot : spot + 8, :] = jnp.where(sub < 4, low, pltpu.roll(high, 4, 0))
            spot += CHUNK
            out[spot : spot + 8, :] = jnp.where(sub < 4, pltpu.roll(low, 4, 0), high)
    zh, c = ids[0:1, :], ids[1:2, :]
    row = lax.broadcasted_iota(jnp.int32, (2, LANES), 0)
    lane = lax.broadcasted_iota(jnp.int32, (2, LANES), 1)
    tile = jnp.zeros((2, LANES), F32)
    for d, ref in zip(LINE, (p0, p1, p2, p3)):
        place = zh ^ d
        value = (ref[...] & (ROWS - 1)).astype(F32)
        value = jnp.broadcast_to(jnp.concatenate([value, value], axis=1), (2, LANES))
        here = (row == (place >> 1)) & ((lane >> 6) == ((place & 1) ^ c))
        tile = jnp.where(here, value, tile)
    for k in range(GROUP):
        out[k * CHUNK + OUTER * 8 : (k + 1) * CHUNK, :] = tile


def gather_kernel(ids, blocks, out, table):
    for high in range(32):
        values = [blocks[(high * 2 + low) * CHUNK + o * 8 : (high * 2 + low) * CHUNK + o * 8 + 8, :] for low in range(2) for o in range(OUTER)]
        for k, value in enumerate(butterfly(values)):
            table[high * 16 + k] = value
    for rest in range(16):
        values = [table[high * 16 + rest] for high in range(32)]
        for high, value in enumerate(butterfly(values)):
            table[high * 16 + rest] = value
    sub = lax.broadcasted_iota(jnp.int32, (8, LANES), 0)
    lane = lax.broadcasted_iota(jnp.int32, (8, LANES), 1)
    upper, first = sub >= 4, lane < SAMP
    zh, half_lane = ids[0:1, :], lane[0:1, :] >> 6
    far = [[((zh >> 1) != zp) & (half_lane == ((zh & 1) ^ c)) for c in range(NC)] for zp in range(2)]
    for half in range(GROUP // 4):
        z0, spot = half // (NQ // 2), half % (NQ // 2) * 8
        for zp in range(2):
            rows = []
            for c in range(NC):
                picked = []
                for ylo in range(2):
                    device = (z0 * NC + c) * NQ + spot // 4 + ylo
                    row = device * CHUNK + OUTER * 8 + zp
                    cross = row + (1 - 2 * z0) * NC * NQ * CHUNK
                    index = jnp.where(far[zp][c], blocks[cross : cross + 1, :], blocks[row : row + 1, :])
                    index = index.astype(jnp.int32)
                    index = jnp.broadcast_to(index, (8, LANES))
                    low = index & (LANES - 1)
                    level = [
                        jnp.take_along_axis(table[device * 8 + o], low, axis=1, mode="promise_in_bounds")
                        for o in range(OUTER)
                    ]
                    for place in range(3):
                        odd = (index & (ORDER << place)) != 0
                        level = [jnp.where(odd, level[k + 1], level[k]) for k in range(0, len(level), 2)]
                    same = ((index & LANES) != 0) == upper
                    picked.append(jnp.where(same, level[0], pltpu.roll(level[0], 4, 0)))
                rows.append(jnp.where(upper, picked[1], picked[0]))
            out[z0, 2 * zp, spot : spot + 8, :] = jnp.where(first, rows[0], rows[1])
            out[z0, 2 * zp + 1, spot : spot + 8, :] = jnp.where(first, rows[1], rows[0])


def zsum_kernel(scale, ids, blocks, out):
    zh = ids[0:1, :]
    odd = jnp.broadcast_to(zh, (8, LANES)) & 1 == 1
    signs = [jnp.broadcast_to(parity_sign(zh & d) * scale, (8, LANES)) for d in range(NZH)]
    for z0 in range(NZ0):
        for spot in range(0, NQ * COLS, 8):
            value = total([blocks[z0, d, spot : spot + 8, :] * signs[d] for d in range(NZH)])
            value = jnp.where(odd, pltpu.roll(value, SAMP, 1), value)
            out[z0 * NQ * COLS + spot : z0 * NQ * COLS + spot + 8, :] = value


def gram_kernel(ids, mine, other, sketch, gram):
    part = NQ * COLS
    zero = jnp.broadcast_to(ids[1:2, :], (part, LANES)) == 0
    pieces = []
    for z0 in range(NZ0):
        a, b = mine[z0 * part : (z0 + 1) * part, :], other[z0 * part : (z0 + 1) * part, :]
        pieces += [jnp.where(zero, a, b), jnp.where(zero, b, a)]
    low, high = jnp.concatenate(pieces[:2], axis=0), jnp.concatenate(pieces[2:], axis=0)
    value = jnp.concatenate([low, high], axis=0)
    zero = jnp.broadcast_to(ids[1:2, :], (W // NC, LANES)) == 0
    gram[...] = lax.dot_general(
        jnp.where(zero, low, high), value, (((1,), (1,)), ((), ())), precision=HIGHEST, preferred_element_type=F32
    )
    for tile, block in enumerate((low, high)):
        turned = block.T
        sketch[:, tile * LANES : (tile + 1) * LANES] = jnp.where(zero[:SAMP], turned[:SAMP], turned[SAMP:])


def spread_kernel(scale, blocks, out):
    value = total([blocks[k] for k in range(blocks.shape[0])]) * scale
    for k in range(out.shape[0]):
        out[k] = value


def factor_kernel(ids, mine, other, rows_in, factor, rows_out, work):
    rows_out[...] = rows_in[...]
    zero = jnp.broadcast_to(ids[1:2, :], (W // NC, LANES)) == 0
    for t in range(W // LANES):
        span = slice(t * LANES, (t + 1) * LANES)
        work[: W // NC, span] = jnp.where(zero, mine[:, span], other[:, span])
        work[W // NC :, span] = jnp.where(zero, other[:, span], mine[:, span])
    sub = lax.broadcasted_iota(jnp.int32, (8, LANES), 0)
    lane = lax.broadcasted_iota(jnp.int32, (8, LANES), 1)
    block = 64
    for top in range(0, W, 8):
        at, tile = top % LANES, top // LANES
        spans = {t: slice(t * LANES, (t + 1) * LANES) for t in range(tile, W // LANES)}
        rows = [
            {t: jnp.broadcast_to(work[top + k : top + k + 1, span], (8, LANES)) for t, span in spans.items()}
            for k in range(8)
        ]
        head = [
            [None] * i + [jnp.broadcast_to(rows[i][tile][:, at + j : at + j + 1], (8, LANES)) for j in range(i, 8)]
            for i in range(8)
        ]
        inverse = []
        for k in range(8):
            inverse.append(lax.rsqrt(head[k][k]))
            for j in range(k + 1, 8):
                head[k][j] = head[k][j] * inverse[k]
            for t in spans:
                rows[k][t] = rows[k][t] * inverse[k]
            for i in range(k + 1, 8):
                for j in range(i, 8):
                    head[i][j] = head[i][j] - head[k][i] * head[k][j]
                for t in spans:
                    rows[i][t] = rows[i][t] - head[k][i] * rows[k][t]
        for t in range(tile):
            factor[top : top + 8, t * LANES : (t + 1) * LANES] = jnp.zeros((8, LANES), F32)
        for t, span in spans.items():
            value = rows[0][t]
            for k in range(1, 8):
                value = jnp.where(sub == k, rows[k][t], value)
            if t == tile:
                value = jnp.where(lane - at >= sub, value, 0.0)
            factor[top : top + 8, span] = value
        first = top // block * block
        last = first + block
        if top + 8 < last:
            for g in range(top + 8, last, 8):
                left = work[g : g + 8, spans[tile]]
                sides = [jnp.broadcast_to(left[:, at + j : at + j + 1], (8, LANES)) for j in range(8)]
                for k in range(8):
                    sides[k] = sides[k] * inverse[k]
                    for j in range(k + 1, 8):
                        sides[j] = sides[j] - sides[k] * head[k][j]
                for t, span in spans.items():
                    work[g : g + 8, span] = work[g : g + 8, span] - total([sides[k] * rows[k][t] for k in range(8)])
        elif last < W:
            start = last // LANES * LANES
            done = factor[first:last, start:]
            for a, b in ((last, last + block), (last + block, W)):
                if a < b:
                    work[a:b, start:] = work[a:b, start:] - lax.dot_general(
                        done[:, a - start : b - start],
                        done,
                        (((0,), (0,)), ((), ())),
                        precision=HIGHEST,
                        preferred_element_type=F32,
                    )


def on_device(matrix, signs, picks):
    zh, c = lax.axis_index("zh"), lax.axis_index("core")
    ids = jnp.broadcast_to(jnp.stack([zh, c]).astype(jnp.int32)[:, None], (2, LANES))
    matrix, ids = lax.optimization_barrier((matrix, ids))
    near = [lax.ppermute(picks, "zh", [(i, i ^ d) for i in range(NZH)]) for d in (1, 3)]
    far = lax.ppermute(picks, ("zh", "z0"), [(i, (i + 3 if i & 1 else i - 3) % NZ) for i in range(NZ)])
    line = [value.reshape(1, SAMP) for value in (picks, near[0], far, near[1])]

    table = pl.pallas_call(
        local_kernel,
        out_shape=shape(OUTER, W, ORDER),
        in_specs=[HBM, HBM],
        out_specs=VMEM,
        scratch_shapes=[
            pltpu.VMEM((ROWS, W), jnp.bfloat16),
            pltpu.VMEM((OUTER * 2, LANES), jnp.int32),
            pltpu.SemaphoreType.DMA((2,)),
            pltpu.SemaphoreType.DMA,
        ],
        compiler_params=params(16),
        name="local",
    )(pinned(matrix), pinned(signs.reshape(OUTER * 2, LANES)))
    packed = pl.pallas_call(
        pack_kernel,
        out_shape=shape(GROUP * CHUNK, LANES),
        in_specs=[VMEM] * 6,
        out_specs=VMEM,
        compiler_params=params(16),
        name="pack",
    )(ids, table, *[line[d] for d in LINE])
    packed = packed.reshape(GROUP, CHUNK // 2, 2, LANES)
    packed = lax.all_to_all(packed, ("z0", "core", "x", "y"), 0, 0, tiled=True).reshape(GROUP * CHUNK, LANES)

    sampled = pl.pallas_call(
        gather_kernel,
        out_shape=shape(NZ0, NZH, NQ * COLS, LANES),
        in_specs=[VMEM] * 2,
        out_specs=VMEM,
        scratch_shapes=[pltpu.VMEM((GROUP * OUTER, 8, LANES), F32)],
        compiler_params=params(16),
        name="gather",
    )(ids, packed)
    sampled = lax.all_to_all(
        sampled.reshape(CHIPS, COLS, LANES), ("z0", "zh", "x", "y"), 0, 0, tiled=True
    ).reshape(NZ0, NZH, NQ * COLS, LANES)

    mine = pl.pallas_call(
        lambda *refs: zsum_kernel(1.0 / math.sqrt(ROWS * 256), *refs),
        out_shape=shape(128, LANES),
        in_specs=[VMEM, VMEM],
        out_specs=VMEM,
        compiler_params=params(4),
        name="zsum",
    )(ids, sampled)
    other = lax.ppermute(mine, "core", [(0, 1), (1, 0)])
    sketch, gram = pl.pallas_call(
        gram_kernel,
        out_shape=[shape(SAMP, W), shape(W // NC, W)],
        in_specs=[VMEM, VMEM, VMEM],
        out_specs=[VMEM, VMEM],
        compiler_params=params(4),
        name="gram",
    )(ids, mine, other)

    def spread(blocks, count, scale, name):
        return pl.pallas_call(
            lambda *refs: spread_kernel(scale, *refs),
            out_shape=shape(count, 8, W),
            in_specs=[VMEM],
            out_specs=VMEM,
            compiler_params=params(4),
            name=name,
        )(blocks)

    gram = lax.all_to_all(gram.reshape(NQ, 8, W), ("x", "y"), 0, 0, tiled=True)
    rows = spread(gram, NZ, 1.0, "sum_xy")
    rows = lax.all_to_all(rows, ("z0", "zh"), 0, 0, tiled=True)
    rows = spread(rows, NQ, 1.0 / (SAMP * 256), "sum_z")
    mine = lax.all_to_all(rows, ("x", "y"), 0, 0, tiled=True).reshape(W // NC, W)
    other = lax.ppermute(mine, "core", [(0, 1), (1, 0)])
    factor, sketch = pl.pallas_call(
        factor_kernel,
        out_shape=[shape(W, W), shape(SAMP, W)],
        in_specs=[VMEM] * 4,
        out_specs=[VMEM, VMEM],
        scratch_shapes=[pltpu.VMEM((W, W), F32)],
        compiler_params=params(4),
        name="factor",
    )(ids, mine, other, sketch)
    return (sketch, factor)


def solution(mesh):
    devices = mesh.devices.transpose([mesh.axis_names.index(name) for name in ("rows", "grp")])
    split = Mesh(devices.reshape(NX, NZH, NZ0, NC, NY), ("x", "zh", "z0", "core", "y"))
    rows = ("y", "x", "zh", "z0", "core")
    return jax.shard_map(
        on_device,
        mesh=split,
        in_specs=(P(rows, None), P(rows), P(rows)),
        out_specs=(P(rows, None), P()),
        check_vma=False,
    )
```
